256 devices in a mesh: aux: 4 (over z_lo), ao: 64 (over z_hi, x, y, core).
Axes of the slice: x: 4, y: 4, z: 8 (z_hi: 2, z_lo: 4; z = z_hi * 4 + z_lo), core: 2. Of those that a mesh axis runs over, the one named last changes fastest.
Arguments:
- half_transformed: bfloat16 [16, 1024, 65536], P('aux', None, 'ao'), may hold values from -1.25 to 1.25
- pair_mask: int32 [512, 6], P('ao'), may hold values 0 or 1
Outputs:
- exchange_tiles: float32 [512, 12, 128, 128], P('ao', None, 'aux')
The draws below stay inside these ranges and needn't reach their ends.
All inputs are finite; a program needn't handle non-finite values. No bound on the sum of `pair_mask` on one device may be relied on, other than what follows from the above.
Results may differ from the reference program's by a relative error of at most 0.012.
Values may be sent and summed in bfloat16 or wider, within the bound.
A program may use at most 128 MiB of HBM per device.

```python
import jax
import jax.numpy as jnp
from jax import lax

Q_DEV = 4
OCC = 1024
BS = 128
W = 6
NB = 512
AO = 65536
Q_ALL = 16
N_AUX = 4


def set_ends(array, rng, smallest, top_value):
    longest = array.shape.index(max(array.shape))
    spots = []
    for shift in (0, 1):
        where = [jax.random.randint(jax.random.fold_in(rng, axis), (), 0, length) for axis, length in enumerate(array.shape)]
        where[longest] = (where[longest] + shift) % array.shape[longest]
        spots.append(tuple(where))
    return array.at[spots[0]].set(smallest).at[spots[1]].set(top_value)


def block_scale(stream_key, shape, cuts, low, largest):
    factor_of = 1.0
    for position, blocks in cuts:
        draws = jax.random.uniform(jax.random.fold_in(jax.random.fold_in(stream_key, 6), position), (blocks,), jnp.float32, low / len(cuts), largest / len(cuts))
        factor_of = factor_of * jnp.repeat(jnp.exp(draws), shape[position] // blocks).reshape((-1,) + (1,) * (len(shape) - 1 - position))
    return factor_of


def normal_values(own_key, shape, width, most, pieces=(), kind=jnp.bfloat16):
    entries = jax.random.normal(own_key, shape, jnp.float32) * width
    if len(pieces) > 0:
        entries = block_scale(own_key, shape, pieces, -0.22, 0.18) * entries
    return jnp.clip(entries, min=-most, max=most).astype(kind)


def setup_inputs(seed: int = 0) -> dict:
    arg_keys = jax.random.split(jax.random.key(seed), 3)
    return {
        "half_transformed": normal_values(arg_keys[0], (Q_ALL, OCC, AO), ((Q_ALL * OCC) ** -0.25), 1.25, ((0, 4), (2, 64))),
        "pair_mask": set_ends((jax.random.randint(arg_keys[1], (NB, W), 0, 2) < 1).astype(jnp.int32), jax.random.fold_in(arg_keys[1], 1), 0, 1),
    }


def reference(half_transformed, pair_mask):
    flat = half_transformed.reshape(N_AUX, Q_DEV * OCC, NB, BS)
    padded = jnp.concatenate([flat, jnp.zeros((N_AUX, Q_DEV * OCC, W, BS), flat.dtype)], axis=2)

    def one_block(index):
        own = lax.dynamic_slice_in_dim(padded, index, 1, 2)[:, :, 0, :].astype(jnp.float32)
        window = lax.dynamic_slice_in_dim(padded, index + 1, W, 2).astype(jnp.float32)
        parts = jnp.einsum("grk,grdl->gdkl", own, window).astype(jnp.bfloat16)
        parts = lax.optimization_barrier(parts)
        return jnp.sum(parts.astype(jnp.float32), axis=0)

    upper = lax.map(one_block, jnp.arange(NB, dtype=jnp.int32))
    upper = upper * (pair_mask > 0).astype(jnp.float32)[:, :, None, None]
    lowers = []
    for offset in range(W, 0, -1):
        moved = jnp.pad(upper[:, offset - 1], ((offset, 0), (0, 0), (0, 0)))[:NB]
        lowers.append(jnp.swapaxes(moved, 1, 2))
    return jnp.concatenate([jnp.stack(lowers, axis=1), upper], axis=1)
```

```python
import functools

import jax
import jax.numpy as jnp
from jax import lax
from jax.experimental import pallas as pl
from jax.experimental.pallas import tpu as pltpu
from jax.sharding import PartitionSpec as P

MESH = pl.DeviceIdType.MESH
BS = 128
W = 6
NBLK = 8
AUX = 4
SL = BS // AUX
KC = 512

INNER = [(i, j) for j in range(1, NBLK) for i in range(max(0, j - W), j)]
INNER_M = [1, 3, 5, 7]
INNER_OFF = [0, 1, 4, 9]
RIGHT = [[(i, b) for i in range(b, W - b)] for b in range(3)]
LEFT = [[(b, j) for j in range(b + 1, W - b)] for b in range(3)]
LO = [1, 2, 3]
HI = [8, 7, 6]


def groups_of(count):
    return (count + 3) // 4


N_IN = len(INNER)
G_IN = groups_of(N_IN)
T0 = [0, N_IN]
for b in range(3):
    T0.append(T0[-1] + len(RIGHT[b]) + len(LEFT[b]))
N_ALL = T0[-1]
GR = [0]
GL = [0]
for b in range(3):
    GR.append(GR[-1] + groups_of(len(RIGHT[b])))
    GL.append(GL[-1] + groups_of(len(LEFT[b])))


def kernel(
    x_hbm, mask_ref, out_ref,
    x, xt, hal, acc, part, rbuf, ts_in, ts_r, ts_l, tr_in, tr_r, tr_l, mask_own, mask_prev,
    load_sem, hs, hr, ms, mr, s1s, s1r, s2s, s2r, crs, crr, cls, clr,
):
    rows = x.shape[0]
    chunks = rows // KC
    n = lax.axis_index("ao")
    a = lax.axis_index("aux")
    n_ao = lax.axis_size("ao")
    has_left = n > 0
    has_right = n < n_ao - 1
    left = jnp.maximum(n - 1, 0)
    right = jnp.minimum(n + 1, n_ao - 1)

    def aux_peer(r):
        return lax.rem(a + r, AUX)

    barrier = pltpu.get_barrier_semaphore()
    for r in range(1, AUX):
        pl.semaphore_signal(barrier, 1, device_id={"aux": aux_peer(r)}, device_id_type=MESH)

    @pl.when(has_left)
    def _():
        for b in range(AUX):
            pl.semaphore_signal(barrier, 1, device_id={"ao": left, "aux": b}, device_id_type=MESH)

    @pl.when(has_right)
    def _():
        for b in range(AUX):
            pl.semaphore_signal(barrier, 1, device_id={"ao": right, "aux": b}, device_id_type=MESH)

    def load(c):
        piece = pl.ds(pl.multiple_of(c * KC, KC), KC)
        return pltpu.make_async_copy(x_hbm.at[piece], x.at[piece], load_sem.at[c])

    for c in range(chunks):
        load(c).start()
    mask_own[...] = jnp.zeros_like(mask_own)
    mask_own[:, 0:W] = mask_ref[...]

    pl.semaphore_wait(
        barrier, AUX - 1 + AUX * (has_left.astype(jnp.int32) + has_right.astype(jnp.int32)))

    def to_left(b):
        return pltpu.make_async_remote_copy(
            x_hbm.at[:, pl.ds(b * BS, BS)], hal.at[b, :, pl.ds(0, BS)],
            hs.at[0, b], hr.at[0, b], device_id={"ao": left}, device_id_type=MESH)

    def to_right(b):
        return pltpu.make_async_remote_copy(
            x_hbm.at[:, pl.ds((NBLK - 1 - b) * BS, BS)], hal.at[b, :, pl.ds(BS, BS)],
            hs.at[1, b], hr.at[1, b], device_id={"ao": right}, device_id_type=MESH)

    mask_copy = pltpu.make_async_remote_copy(
        mask_own, mask_prev, ms, mr, device_id={"ao": right}, device_id_type=MESH)

    @pl.when(has_right)
    def _():
        mask_copy.start()

    for b in range(3):
        @pl.when(has_left)
        def _():
            to_left(b).start()

        @pl.when(has_right)
        def _():
            to_right(b).start()

    @pl.when(jnp.logical_not(has_left))
    def _():
        hal[:, :, BS:] = jnp.zeros((3, rows, BS), hal.dtype)
        tr_r[...] = jnp.zeros_like(tr_r)
        mask_prev[...] = jnp.zeros_like(mask_prev)

    @pl.when(jnp.logical_not(has_right))
    def _():
        hal[:, :, :BS] = jnp.zeros((3, rows, BS), hal.dtype)
        tr_l[...] = jnp.zeros_like(tr_l)

    acc[...] = jnp.zeros_like(acc)

    def inner_step(c, carry):
        load(c).wait()
        piece = pl.ds(pl.multiple_of(c * KC, KC), KC)
        for b in range(NBLK):
            xt[c, b * BS:(b + 1) * BS, :] = x[piece, b * BS:(b + 1) * BS].T
        for q in range(4):
            lhs = xt[c, 0:INNER_M[q] * BS, :]
            rhs = x[piece, 2 * q * BS:(2 * q + 2) * BS]
            where = slice(INNER_OFF[q] * BS, (INNER_OFF[q] + INNER_M[q]) * BS)
            acc[where, :] += jnp.dot(lhs, rhs, preferred_element_type=jnp.float32)
        return carry

    lax.fori_loop(0, chunks, inner_step, 0)

    def put(tile, keep, t):
        scaled = tile * (keep > 0).astype(jnp.float32)
        part[:, t] = scaled.astype(part.dtype).reshape(AUX, SL, BS)

    for t, (i, j) in enumerate(INNER):
        row = (INNER_OFF[j // 2] + i) * BS
        col = (j % 2) * BS
        put(acc[row:row + BS, col:col + BS], mask_own[i:i + 1, j - i - 1:j - i], t)

    def send1(k, r):
        span = pl.ds(T0[k], T0[k + 1] - T0[k])
        return pltpu.make_async_remote_copy(
            part.at[aux_peer(r), span], rbuf.at[r - 1, span],
            s1s.at[k, r - 1], s1r.at[k, r - 1], device_id={"aux": aux_peer(r)}, device_id_type=MESH)

    for r in range(1, AUX):
        send1(0, r).start()

    def cross(b):
        @pl.when(has_right)
        def _():
            to_left(b).wait_recv()

        @pl.when(has_left)
        def _():
            to_right(b).wait_recv()

        if b == 0:
            @pl.when(has_left)
            def _():
                mask_copy.wait_recv()

        lo, size = LO[b] * BS, (HI[b] - LO[b]) * BS
        acc[0:size, :] = jnp.zeros((size, 2 * BS), jnp.float32)

        def step(c, carry):
            piece = pl.ds(pl.multiple_of(c * KC, KC), KC)
            acc[0:size, :] += jnp.dot(
                xt[c, lo:lo + size, :], hal[b, piece, :], preferred_element_type=jnp.float32)
            return carry

        lax.fori_loop(0, chunks, step, 0)
        t = T0[b + 1]
        for i, j in RIGHT[b]:
            own = NBLK - 1 - i
            row = (own - LO[b]) * BS
            put(acc[row:row + BS, 0:BS], mask_own[own:own + 1, i + j:i + j + 1], t)
            t += 1
        for i, j in LEFT[b]:
            row = (j - LO[b]) * BS
            far = NBLK - 1 - i
            put(acc[row:row + BS, BS:2 * BS], mask_prev[far:far + 1, i + j:i + j + 1], t)
            t += 1
        for r in range(1, AUX):
            send1(b + 1, r).start()

    def total(t):
        value = part[a, t].astype(jnp.float32)
        for r in range(1, AUX):
            value = value + rbuf[r - 1, t].astype(jnp.float32)
        return value

    def turn(values, ts, g):
        values = values + [jnp.zeros((SL, BS), jnp.float32)] * (4 - len(values))
        ts[:, g] = jnp.concatenate(values, axis=0).T.astype(ts.dtype).reshape(AUX, SL, BS)

    def sums(t0, places, ts, g0):
        for g in range(groups_of(len(places))):
            values = []
            for u, (m, e) in enumerate(places[4 * g:4 * g + 4]):
                value = total(t0 + 4 * g + u)
                out_ref[m, e] = value
                values.append(value)
            turn(values, ts, g0 + g)

    def send_in(r):
        return pltpu.make_async_remote_copy(
            ts_in.at[aux_peer(r)], tr_in.at[a], s2s.at[r - 1], s2r.at[r - 1],
            device_id={"aux": aux_peer(r)}, device_id_type=MESH)

    def send_r(b, to):
        span = pl.ds(GR[b], GR[b + 1] - GR[b])
        return pltpu.make_async_remote_copy(
            ts_r.at[to, span], tr_r.at[a, span], crs.at[b, to], crr.at[b, a],
            device_id={"ao": right, "aux": to}, device_id_type=MESH)

    def send_l(b, to):
        span = pl.ds(GL[b], GL[b + 1] - GL[b])
        return pltpu.make_async_remote_copy(
            ts_l.at[to, span], tr_l.at[a, span], cls.at[b, to], clr.at[b, a],
            device_id={"ao": left, "aux": to}, device_id_type=MESH)

    def got_r(b, source):
        span = pl.ds(GR[b], GR[b + 1] - GR[b])
        return pltpu.make_async_remote_copy(
            ts_r.at[source, span], tr_r.at[source, span], crs.at[b, source], crr.at[b, source],
            device_id={"ao": left, "aux": source}, device_id_type=MESH)

    def got_l(b, source):
        span = pl.ds(GL[b], GL[b + 1] - GL[b])
        return pltpu.make_async_remote_copy(
            ts_l.at[source, span], tr_l.at[source, span], cls.at[b, source], clr.at[b, source],
            device_id={"ao": right, "aux": source}, device_id_type=MESH)

    def inner_sums():
        for r in range(1, AUX):
            send1(0, r).wait_recv()
        sums(0, [(i, W + j - i - 1) for i, j in INNER], ts_in, 0)
        tr_in[a] = ts_in[a]
        for r in range(1, AUX):
            send_in(r).start()

    def cross_sums(b):
        for r in range(1, AUX):
            send1(b + 1, r).wait_recv()
        t = T0[b + 1]
        sums(t, [(NBLK - 1 - i, W + i + j) for i, j in RIGHT[b]], ts_r, GR[b])

        @pl.when(has_right)
        def _():
            for to in range(AUX):
                send_r(b, to).start()

        sums(t + len(RIGHT[b]), [(j, W - 1 - i - j) for i, j in LEFT[b]], ts_l, GL[b])

        @pl.when(has_left)
        def _():
            for to in range(AUX):
                send_l(b, to).start()

    def place(tr, g0, places):
        for u, (m, e) in enumerate(places):
            g, v = g0 + u // 4, u % 4
            pieces = [tr[source, g, :, v * SL:(v + 1) * SL].astype(jnp.float32) for source in range(AUX)]
            out_ref[m, e] = jnp.concatenate(pieces, axis=1)

    def inner_place():
        for r in range(1, AUX):
            send_in(r).wait_recv()
        place(tr_in, 0, [(j, W - (j - i)) for i, j in INNER])

    def cross_place(b):
        @pl.when(has_left)
        def _():
            for source in range(AUX):
                got_r(b, source).wait_recv()

        place(tr_r, GR[b], [(j, W - 1 - i - j) for i, j in RIGHT[b]])

        @pl.when(has_right)
        def _():
            for source in range(AUX):
                got_l(b, source).wait_recv()

        place(tr_l, GL[b], [(NBLK - 1 - i, W + i + j) for i, j in LEFT[b]])

    cross(0)
    cross(1)
    inner_sums()
    cross_sums(0)
    cross(2)
    cross_sums(1)
    inner_place()
    cross_place(0)
    cross_sums(2)
    cross_place(1)
    cross_place(2)

    for k in range(4):
        for r in range(1, AUX):
            send1(k, r).wait_send()
    for r in range(1, AUX):
        send_in(r).wait_send()

    @pl.when(has_right)
    def _():
        mask_copy.wait_send()
        for b in range(3):
            to_right(b).wait_send()
            for to in range(AUX):
                send_r(b, to).wait_send()

    @pl.when(has_left)
    def _():
        for b in range(3):
            to_left(b).wait_send()
            for to in range(AUX):
                send_l(b, to).wait_send()


def body(half_transformed, pair_mask):
    flat = half_transformed.reshape(-1, NBLK * BS)
    rows = flat.shape[0]
    bf16 = jnp.bfloat16
    dma = pltpu.SemaphoreType.DMA
    return pl.pallas_call(
        kernel,
        out_shape=jax.ShapeDtypeStruct((NBLK, 2 * W, SL, BS), jnp.float32),
        in_specs=[pl.BlockSpec(memory_space=pl.ANY), pl.BlockSpec(memory_space=pltpu.VMEM)],
        out_specs=pl.BlockSpec(memory_space=pltpu.VMEM),
        scratch_shapes=[
            pltpu.VMEM((rows, NBLK * BS), bf16),
            pltpu.VMEM((rows // KC, NBLK * BS, KC), bf16),
            pltpu.VMEM((3, rows, 2 * BS), bf16),
            pltpu.VMEM((sum(INNER_M) * BS, 2 * BS), jnp.float32),
            pltpu.VMEM((AUX, N_ALL, SL, BS), bf16),
            pltpu.VMEM((AUX - 1, N_ALL, SL, BS), bf16),
            pltpu.VMEM((AUX, G_IN, SL, BS), bf16),
            pltpu.VMEM((AUX, GR[3], SL, BS), bf16),
            pltpu.VMEM((AUX, GL[3], SL, BS), bf16),
            pltpu.VMEM((AUX, G_IN, SL, BS), bf16),
            pltpu.VMEM((AUX, GR[3], SL, BS), bf16),
            pltpu.VMEM((AUX, GL[3], SL, BS), bf16),
            pltpu.VMEM((NBLK, BS), jnp.int32),
            pltpu.VMEM((NBLK, BS), jnp.int32),
            dma((rows // KC,)),
            dma((2, 3)), dma((2, 3)),
            dma, dma,
            dma((4, AUX - 1)), dma((4, AUX - 1)),
            dma((AUX - 1,)), dma((AUX - 1,)),
            dma((3, AUX)), dma((3, AUX)),
            dma((3, AUX)), dma((3, AUX)),
        ],
        compiler_params=pltpu.CompilerParams(
            collective_id=0, has_side_effects=True, vmem_limit_bytes=48 << 20),
        cost_estimate=pl.CostEstimate(flops=8 << 30, bytes_accessed=16 << 20, transcendentals=0),
    )(flat, pair_mask)


def solution(mesh):
    return jax.shard_map(
        body,
        mesh=mesh,
        in_specs=(P("aux", None, "ao"), P("ao", None)),
        out_specs=P("ao", None, "aux", None),
        check_vma=False,
    )
```

```python
import functools

import jax
import jax.numpy as jnp
from jax import lax
from jax.experimental import pallas as pl
from jax.experimental.pallas import tpu as pltpu
from jax.sharding import PartitionSpec as P

MESH = pl.DeviceIdType.MESH
BS = 128
W = 6
NBLK = 8
AUX = 4
SL = BS // AUX
KC = 512
SEAM = 31
RELAY = [7, 15, 0]

INNER = [(i, j) for j in range(1, NBLK) for i in range(max(0, j - W), j)]
INNER_M = [1, 3, 5, 7]
INNER_OFF = [0, 1, 4, 9]
RIGHT = [[(i, b) for i in range(b, W - b)] for b in range(3)]
LEFT = [[(b, j) for j in range(b + 1, W - b)] for b in range(3)]
LO = [1, 2, 3]
HI = [8, 7, 6]


def groups_of(count):
    return (count + 3) // 4


N_IN = len(INNER)
G_IN = groups_of(N_IN)
T0 = [0, N_IN]
for b in range(3):
    T0.append(T0[-1] + len(RIGHT[b]) + len(LEFT[b]))
N_ALL = T0[-1]
GR = [0]
GL = [0]
for b in range(3):
    GR.append(GR[-1] + groups_of(len(RIGHT[b])))
    GL.append(GL[-1] + groups_of(len(LEFT[b])))


def kernel(
    x_hbm, mask_ref, out_ref,
    x, xt, hal, rel, acc, part, rbuf, ts_in, ts_r, ts_l, tr_in, tr_r, tr_l, mask_own, mask_prev,
    load_sem, hs, hr, ss, sr, rs, rr, ms, mr, s1s, s1r, s2s, s2r, crs, crr, cls, clr,
):
    rows = x.shape[0]
    chunks = rows // KC
    n = lax.axis_index("ao")
    a = lax.axis_index("aux")
    n_ao = lax.axis_size("ao")
    fwd = n <= SEAM
    at_seam = (n == SEAM) | (n == SEAM + 1)
    last = n_ao - 1
    has_left = n > 0
    has_right = n < n_ao - 1
    left = jnp.maximum(n - 1, 0)
    right = jnp.minimum(n + 1, n_ao - 1)

    def aux_peer(r):
        return lax.rem(a + r, AUX)

    barrier = pltpu.get_barrier_semaphore()
    for r in range(1, AUX):
        pl.semaphore_signal(barrier, 1, device_id={"aux": aux_peer(r)}, device_id_type=MESH)

    @pl.when(has_left)
    def _():
        for b in range(AUX):
            pl.semaphore_signal(barrier, 1, device_id={"ao": left, "aux": b}, device_id_type=MESH)

    @pl.when(has_right)
    def _():
        for b in range(AUX):
            pl.semaphore_signal(barrier, 1, device_id={"ao": right, "aux": b}, device_id_type=MESH)

    quarter = rows // AUX

    def relay_of(p):
        return jnp.where(fwd, RELAY[p - 1], last - RELAY[p - 1])

    def is_relay(p):
        return n == relay_of(p)

    relay_to = jnp.where(fwd, SEAM + 1, SEAM)
    relay_from = jnp.where(fwd, SEAM, SEAM + 1)
    extra = jnp.where(at_seam, AUX - 1, 0)
    for p in range(1, AUX):
        extra += jnp.where(is_relay(p), 1, 0)

        @pl.when(is_relay(p))
        def _():
            pl.semaphore_signal(barrier, 1, device_id={"ao": relay_from}, device_id_type=MESH)

        @pl.when(at_seam)
        def _():
            other = jnp.where(fwd, last - RELAY[p - 1], RELAY[p - 1])
            pl.semaphore_signal(barrier, 1, device_id={"ao": other}, device_id_type=MESH)

    def load(c):
        piece = pl.ds(pl.multiple_of(c * KC, KC), KC)
        return pltpu.make_async_copy(x_hbm.at[piece], x.at[piece], load_sem.at[c])

    for c in range(chunks):
        load(c).start()
    mask_own[...] = jnp.zeros_like(mask_own)
    mask_own[:, 0:W] = mask_ref[...]

    pl.semaphore_wait(
        barrier, AUX - 1 + AUX * (has_left.astype(jnp.int32) + has_right.astype(jnp.int32)) + extra)

    def to_left(b):
        return pltpu.make_async_remote_copy(
            x_hbm.at[:, pl.ds(b * BS, BS)], hal.at[b, :, pl.ds(0, BS)],
            hs.at[0, b], hr.at[0, b], device_id={"ao": left}, device_id_type=MESH)

    def to_right(b):
        return pltpu.make_async_remote_copy(
            x_hbm.at[:, pl.ds((NBLK - 1 - b) * BS, BS)], hal.at[b, :, pl.ds(BS, BS)],
            hs.at[1, b], hr.at[1, b], device_id={"ao": right}, device_id_type=MESH)

    def seam_span(p, lanes):
        return (pl.ds(p * quarter, quarter), pl.ds(pl.multiple_of(lanes, BS), BS))

    def seam_out(b, p):
        source = x_hbm.at[seam_span(p, jnp.where(fwd, (NBLK - 1 - b) * BS, b * BS))]
        if p == 0:
            return pltpu.make_async_remote_copy(
                source, hal.at[(b,) + seam_span(p, jnp.where(fwd, BS, 0))],
                ss.at[p, b], sr.at[p, b], device_id={"ao": relay_to}, device_id_type=MESH)
        return pltpu.make_async_remote_copy(
            source, rel.at[b], ss.at[p, b], rr.at[b], device_id={"ao": relay_of(p)}, device_id_type=MESH)

    def relay_out(b, p):
        return pltpu.make_async_remote_copy(
            rel.at[b], hal.at[(b,) + seam_span(p, jnp.where(fwd, BS, 0))],
            rs.at[b], sr.at[p, b], device_id={"ao": relay_to}, device_id_type=MESH)

    def seam_in(b, p):
        return pltpu.make_async_remote_copy(
            rel.at[b], hal.at[(b,) + seam_span(p, jnp.where(fwd, 0, BS))],
            rs.at[b], sr.at[p, b], device_id={"ao": relay_to}, device_id_type=MESH)

    def relay(b):
        for p in range(1, AUX):
            @pl.when(is_relay(p))
            def _():
                seam_out(b, p).wait_recv()
                relay_out(b, p).start()

    near_left = has_left & (n != SEAM + 1)
    near_right = has_right & (n != SEAM)
    mask_copy = pltpu.make_async_remote_copy(
        mask_own, mask_prev, ms, mr, device_id={"ao": right}, device_id_type=MESH)

    @pl.when(has_right)
    def _():
        mask_copy.start()

    for b in range(3):
        @pl.when(near_left)
        def _():
            to_left(b).start()

        @pl.when(near_right)
        def _():
            to_right(b).start()

        @pl.when(at_seam)
        def _():
            for p in (1, 3, 2, 0):
                seam_out(b, p).start()

    @pl.when(jnp.logical_not(has_left))
    def _():
        hal[:, :, BS:] = jnp.zeros((3, rows, BS), hal.dtype)
        tr_r[...] = jnp.zeros_like(tr_r)
        mask_prev[...] = jnp.zeros_like(mask_prev)

    @pl.when(jnp.logical_not(has_right))
    def _():
        hal[:, :, :BS] = jnp.zeros((3, rows, BS), hal.dtype)
        tr_l[...] = jnp.zeros_like(tr_l)

    acc[...] = jnp.zeros_like(acc)

    def inner_step(c, carry):
        load(c).wait()
        piece = pl.ds(pl.multiple_of(c * KC, KC), KC)
        for b in range(NBLK):
            xt[c, b * BS:(b + 1) * BS, :] = x[piece, b * BS:(b + 1) * BS].T
        for q in range(4):
            lhs = xt[c, 0:INNER_M[q] * BS, :]
            rhs = x[piece, 2 * q * BS:(2 * q + 2) * BS]
            where = slice(INNER_OFF[q] * BS, (INNER_OFF[q] + INNER_M[q]) * BS)
            acc[where, :] += jnp.dot(lhs, rhs, preferred_element_type=jnp.float32)
        return carry

    lax.fori_loop(0, chunks, inner_step, 0)
    relay(0)

    def put(tile, keep, t):
        scaled = tile * (keep > 0).astype(jnp.float32)
        part[:, t] = scaled.astype(part.dtype).reshape(AUX, SL, BS)

    for t, (i, j) in enumerate(INNER):
        row = (INNER_OFF[j // 2] + i) * BS
        col = (j % 2) * BS
        put(acc[row:row + BS, col:col + BS], mask_own[i:i + 1, j - i - 1:j - i], t)

    def send1(k, r):
        span = pl.ds(T0[k], T0[k + 1] - T0[k])
        return pltpu.make_async_remote_copy(
            part.at[aux_peer(r), span], rbuf.at[r - 1, span],
            s1s.at[k, r - 1], s1r.at[k, r - 1], device_id={"aux": aux_peer(r)}, device_id_type=MESH)

    for r in range(1, AUX):
        send1(0, r).start()

    def cross(b):
        @pl.when(near_right)
        def _():
            to_left(b).wait_recv()

        @pl.when(near_left)
        def _():
            to_right(b).wait_recv()

        @pl.when(at_seam)
        def _():
            for p in range(AUX):
                seam_in(b, p).wait_recv()

        if b == 0:
            @pl.when(has_left)
            def _():
                mask_copy.wait_recv()

        lo, size = LO[b] * BS, (HI[b] - LO[b]) * BS
        acc[0:size, :] = jnp.zeros((size, 2 * BS), jnp.float32)

        def step(c, carry):
            piece = pl.ds(pl.multiple_of(c * KC, KC), KC)
            acc[0:size, :] += jnp.dot(
                xt[c, lo:lo + size, :], hal[b, piece, :], preferred_element_type=jnp.float32)
            return carry

        lax.fori_loop(0, chunks, step, 0)
        t = T0[b + 1]
        for i, j in RIGHT[b]:
            own = NBLK - 1 - i
            row = (own - LO[b]) * BS
            put(acc[row:row + BS, 0:BS], mask_own[own:own + 1, i + j:i + j + 1], t)
            t += 1
        for i, j in LEFT[b]:
            row = (j - LO[b]) * BS
            far = NBLK - 1 - i
            put(acc[row:row + BS, BS:2 * BS], mask_prev[far:far + 1, i + j:i + j + 1], t)
            t += 1
        for r in range(1, AUX):
            send1(b + 1, r).start()

    def total(t):
        value = part[a, t].astype(jnp.float32)
        for r in range(1, AUX):
            value = value + rbuf[r - 1, t].astype(jnp.float32)
        return value

    def turn(values, ts, g):
        values = values + [jnp.zeros((SL, BS), jnp.float32)] * (4 - len(values))
        ts[:, g] = jnp.concatenate(values, axis=0).T.astype(ts.dtype).reshape(AUX, SL, BS)

    def sums(t0, places, ts, g0):
        for g in range(groups_of(len(places))):
            values = []
            for u, (m, e) in enumerate(places[4 * g:4 * g + 4]):
                value = total(t0 + 4 * g + u)
                out_ref[m, e] = value
                values.append(value)
            turn(values, ts, g0 + g)

    def send_in(r):
        return pltpu.make_async_remote_copy(
            ts_in.at[aux_peer(r)], tr_in.at[a], s2s.at[r - 1], s2r.at[r - 1],
            device_id={"aux": aux_peer(r)}, device_id_type=MESH)

    def send_r(b, to):
        span = pl.ds(GR[b], GR[b + 1] - GR[b])
        return pltpu.make_async_remote_copy(
            ts_r.at[to, span], tr_r.at[a, span], crs.at[b, to], crr.at[b, a],
            device_id={"ao": right, "aux": to}, device_id_type=MESH)

    def send_l(b, to):
        span = pl.ds(GL[b], GL[b + 1] - GL[b])
        return pltpu.make_async_remote_copy(
            ts_l.at[to, span], tr_l.at[a, span], cls.at[b, to], clr.at[b, a],
            device_id={"ao": left, "aux": to}, device_id_type=MESH)

    def got_r(b, source):
        span = pl.ds(GR[b], GR[b + 1] - GR[b])
        return pltpu.make_async_remote_copy(
            ts_r.at[source, span], tr_r.at[source, span], crs.at[b, source], crr.at[b, source],
            device_id={"ao": left, "aux": source}, device_id_type=MESH)

    def got_l(b, source):
        span = pl.ds(GL[b], GL[b + 1] - GL[b])
        return pltpu.make_async_remote_copy(
            ts_l.at[source, span], tr_l.at[source, span], cls.at[b, source], clr.at[b, source],
            device_id={"ao": right, "aux": source}, device_id_type=MESH)

    def inner_sums():
        for r in range(1, AUX):
            send1(0, r).wait_recv()
        sums(0, [(i, W + j - i - 1) for i, j in INNER], ts_in, 0)
        tr_in[a] = ts_in[a]
        for r in range(1, AUX):
            send_in(r).start()

    def cross_sums(b):
        for r in range(1, AUX):
            send1(b + 1, r).wait_recv()
        t = T0[b + 1]
        sums(t, [(NBLK - 1 - i, W + i + j) for i, j in RIGHT[b]], ts_r, GR[b])

        @pl.when(has_right)
        def _():
            for to in range(AUX):
                send_r(b, to).start()

        sums(t + len(RIGHT[b]), [(j, W - 1 - i - j) for i, j in LEFT[b]], ts_l, GL[b])

        @pl.when(has_left)
        def _():
            for to in range(AUX):
                send_l(b, to).start()

    def place(tr, g0, places):
        for u, (m, e) in enumerate(places):
            g, v = g0 + u // 4, u % 4
            pieces = [tr[source, g, :, v * SL:(v + 1) * SL].astype(jnp.float32) for source in range(AUX)]
            out_ref[m, e] = jnp.concatenate(pieces, axis=1)

    def inner_place():
        for r in range(1, AUX):
            send_in(r).wait_recv()
        place(tr_in, 0, [(j, W - (j - i)) for i, j in INNER])

    def cross_place(b):
        @pl.when(has_left)
        def _():
            for source in range(AUX):
                got_r(b, source).wait_recv()

        place(tr_r, GR[b], [(j, W - 1 - i - j) for i, j in RIGHT[b]])

        @pl.when(has_right)
        def _():
            for source in range(AUX):
                got_l(b, source).wait_recv()

        place(tr_l, GL[b], [(NBLK - 1 - i, W + i + j) for i, j in LEFT[b]])

    relay(1)
    cross(0)
    relay(2)
    cross(1)
    inner_sums()
    cross_sums(0)
    cross(2)
    cross_sums(1)
    inner_place()
    cross_place(0)
    cross_sums(2)
    cross_place(1)
    cross_place(2)

    for k in range(4):
        for r in range(1, AUX):
            send1(k, r).wait_send()
    for r in range(1, AUX):
        send_in(r).wait_send()

    @pl.when(has_right)
    def _():
        mask_copy.wait_send()
        for b in range(3):
            for to in range(AUX):
                send_r(b, to).wait_send()

    @pl.when(has_left)
    def _():
        for b in range(3):
            for to in range(AUX):
                send_l(b, to).wait_send()

    for b in range(3):
        @pl.when(near_right)
        def _():
            to_right(b).wait_send()

        @pl.when(near_left)
        def _():
            to_left(b).wait_send()

        @pl.when(at_seam)
        def _():
            for p in range(AUX):
                seam_out(b, p).wait_send()

        for p in range(1, AUX):
            @pl.when(is_relay(p))
            def _():
                relay_out(b, p).wait_send()


def body(half_transformed, pair_mask):
    flat = half_transformed.reshape(-1, NBLK * BS)
    rows = flat.shape[0]
    bf16 = jnp.bfloat16
    dma = pltpu.SemaphoreType.DMA
    return pl.pallas_call(
        kernel,
        out_shape=jax.ShapeDtypeStruct((NBLK, 2 * W, SL, BS), jnp.float32),
        in_specs=[pl.BlockSpec(memory_space=pl.ANY), pl.BlockSpec(memory_space=pltpu.VMEM)],
        out_specs=pl.BlockSpec(memory_space=pltpu.VMEM),
        scratch_shapes=[
            pltpu.VMEM((rows, NBLK * BS), bf16),
            pltpu.VMEM((rows // KC, NBLK * BS, KC), bf16),
            pltpu.VMEM((3, rows, 2 * BS), bf16),
            pltpu.VMEM((3, rows // AUX, BS), bf16),
            pltpu.VMEM((sum(INNER_M) * BS, 2 * BS), jnp.float32),
            pltpu.VMEM((AUX, N_ALL, SL, BS), bf16),
            pltpu.VMEM((AUX - 1, N_ALL, SL, BS), bf16),
            pltpu.VMEM((AUX, G_IN, SL, BS), bf16),
            pltpu.VMEM((AUX, GR[3], SL, BS), bf16),
            pltpu.VMEM((AUX, GL[3], SL, BS), bf16),
            pltpu.VMEM((AUX, G_IN, SL, BS), bf16),
            pltpu.VMEM((AUX, GR[3], SL, BS), bf16),
            pltpu.VMEM((AUX, GL[3], SL, BS), bf16),
            pltpu.VMEM((NBLK, BS), jnp.int32),
            pltpu.VMEM((NBLK, BS), jnp.int32),
            dma((rows // KC,)),
            dma((2, 3)), dma((2, 3)),
            dma((AUX, 3)), dma((AUX, 3)), dma((3,)), dma((3,)),
            dma, dma,
            dma((4, AUX - 1)), dma((4, AUX - 1)),
            dma((AUX - 1,)), dma((AUX - 1,)),
            dma((3, AUX)), dma((3, AUX)),
            dma((3, AUX)), dma((3, AUX)),
        ],
        compiler_params=pltpu.CompilerParams(
            collective_id=0, has_side_effects=True, vmem_limit_bytes=48 << 20),
        cost_estimate=pl.CostEstimate(flops=8 << 30, bytes_accessed=16 << 20, transcendentals=0),
    )(flat, pair_mask)


def solution(mesh):
    return jax.shard_map(
        body,
        mesh=mesh,
        in_specs=(P("aux", None, "ao"), P("ao", None)),
        out_specs=P("ao", None, "aux", None),
        check_vma=False,
    )
```

```python
import functools

import jax
import jax.numpy as jnp
from jax import lax
from jax.experimental import pallas as pl
from jax.experimental.pallas import tpu as pltpu
from jax.sharding import PartitionSpec as P

MESH = pl.DeviceIdType.MESH
BS = 128
W = 6
NBLK = 8
AUX = 4
SL = BS // AUX
KC = 1024
SEAM = 31
RELAY = [7, 15, 0]

INNER = [(i, j) for j in range(1, NBLK) for i in range(max(0, j - W), j)]
INNER_M = [1, 3, 5, 7]
INNER_OFF = [0, 1, 4, 9]
RIGHT = [[(i, b) for i in range(b, W - b)] for b in range(3)]
LEFT = [[(b, j) for j in range(b + 1, W - b)] for b in range(3)]
LO = [1, 2, 3]
HI = [8, 7, 6]


def groups_of(count):
    return (count + 3) // 4


EARLY = 15
INNER_PART = [INNER[:EARLY], INNER[EARLY:]]
T0 = [0, EARLY, len(INNER)]
for b in range(3):
    T0.append(T0[-1] + len(RIGHT[b]) + len(LEFT[b]))
N_ALL = T0[-1]
TAIL = T0[4]
GI = [0, groups_of(EARLY), groups_of(EARLY) + groups_of(len(INNER) - EARLY)]
GR = [0]
GL = [0]
for b in range(2):
    GR.append(GR[-1] + groups_of(len(RIGHT[b])))
    GL.append(GL[-1] + groups_of(len(LEFT[b])))


def kernel(
    x_hbm, mask_ref, out_ref,
    x, xt, hal, rel, acc, part, own_sum, far_sum, far_out, far_in, tail_in,
    ts_in, ts_r, ts_l, tr_in, tr_r, tr_l, tail_r, tail_l, tail_r_in, tail_l_in, mask_own, mask_prev,
    load_sem, hs, hr, ss, sr, rs, rr, ms, mr,
    os, orr, fs, fr, gs, gr, ds, dr, s2s, s2r, crs, crr, cls, clr,
):
    rows = x.shape[0]
    chunks = rows // KC
    n = lax.axis_index("ao")
    a = lax.axis_index("aux")
    n_ao = lax.axis_size("ao")
    fwd = n <= SEAM
    at_seam = (n == SEAM) | (n == SEAM + 1)
    last = n_ao - 1
    has_left = n > 0
    has_right = n < n_ao - 1
    pair = a + 1 - 2 * lax.rem(a, 2)
    mirror = AUX - 1 - a
    left = jnp.maximum(n - 1, 0)
    right = jnp.minimum(n + 1, n_ao - 1)

    def aux_peer(r):
        return lax.rem(a + r, AUX)

    barrier = pltpu.get_barrier_semaphore()
    for r in range(1, AUX):
        pl.semaphore_signal(barrier, 1, device_id={"aux": aux_peer(r)}, device_id_type=MESH)

    @pl.when(has_left)
    def _():
        for b in range(AUX):
            pl.semaphore_signal(barrier, 1, device_id={"ao": left, "aux": b}, device_id_type=MESH)

    @pl.when(has_right)
    def _():
        for b in range(AUX):
            pl.semaphore_signal(barrier, 1, device_id={"ao": right, "aux": b}, device_id_type=MESH)

    quarter = rows // AUX

    def relay_of(p):
        return jnp.where(fwd, RELAY[p - 1], last - RELAY[p - 1])

    def is_relay(p):
        return n == relay_of(p)

    relay_to = jnp.where(fwd, SEAM + 1, SEAM)
    relay_from = jnp.where(fwd, SEAM, SEAM + 1)
    extra = jnp.where(at_seam, AUX - 1, 0)
    for p in range(1, AUX):
        extra += jnp.where(is_relay(p), 1, 0)

        @pl.when(is_relay(p))
        def _():
            pl.semaphore_signal(barrier, 1, device_id={"ao": relay_from}, device_id_type=MESH)

        @pl.when(at_seam)
        def _():
            other = jnp.where(fwd, last - RELAY[p - 1], RELAY[p - 1])
            pl.semaphore_signal(barrier, 1, device_id={"ao": other}, device_id_type=MESH)

    def load(c):
        piece = pl.ds(pl.multiple_of(c * KC, KC), KC)
        return pltpu.make_async_copy(x_hbm.at[piece], x.at[piece], load_sem.at[c])

    for c in range(chunks):
        load(c).start()
    mask_own[...] = jnp.zeros_like(mask_own)
    mask_own[:, 0:W] = mask_ref[...]

    pl.semaphore_wait(
        barrier, AUX - 1 + AUX * (has_left.astype(jnp.int32) + has_right.astype(jnp.int32)) + extra)

    def to_left(b):
        return pltpu.make_async_remote_copy(
            x_hbm.at[:, pl.ds(b * BS, BS)], hal.at[b, :, pl.ds(0, BS)],
            hs.at[0, b], hr.at[0, b], device_id={"ao": left}, device_id_type=MESH)

    def to_right(b):
        return pltpu.make_async_remote_copy(
            x_hbm.at[:, pl.ds((NBLK - 1 - b) * BS, BS)], hal.at[b, :, pl.ds(BS, BS)],
            hs.at[1, b], hr.at[1, b], device_id={"ao": right}, device_id_type=MESH)

    def seam_span(p, lanes):
        return (pl.ds(p * quarter, quarter), pl.ds(pl.multiple_of(lanes, BS), BS))

    def seam_out(b, p):
        source = x_hbm.at[seam_span(p, jnp.where(fwd, (NBLK - 1 - b) * BS, b * BS))]
        if p == 0:
            return pltpu.make_async_remote_copy(
                source, hal.at[(b,) + seam_span(p, jnp.where(fwd, BS, 0))],
                ss.at[p, b], sr.at[p, b], device_id={"ao": relay_to}, device_id_type=MESH)
        return pltpu.make_async_remote_copy(
            source, rel.at[b], ss.at[p, b], rr.at[b], device_id={"ao": relay_of(p)}, device_id_type=MESH)

    def relay_out(b, p):
        return pltpu.make_async_remote_copy(
            rel.at[b], hal.at[(b,) + seam_span(p, jnp.where(fwd, BS, 0))],
            rs.at[b], sr.at[p, b], device_id={"ao": relay_to}, device_id_type=MESH)

    def seam_in(b, p):
        return pltpu.make_async_remote_copy(
            rel.at[b], hal.at[(b,) + seam_span(p, jnp.where(fwd, 0, BS))],
            rs.at[b], sr.at[p, b], device_id={"ao": relay_to}, device_id_type=MESH)

    def relay(b):
        for p in range(1, AUX):
            @pl.when(is_relay(p))
            def _():
                seam_out(b, p).wait_recv()
                relay_out(b, p).start()

    near_left = has_left & (n != SEAM + 1)
    near_right = has_right & (n != SEAM)
    mask_copy = pltpu.make_async_remote_copy(
        mask_own, mask_prev, ms, mr, device_id={"ao": right}, device_id_type=MESH)

    @pl.when(has_right)
    def _():
        mask_copy.start()

    for b in range(3):
        @pl.when(near_left)
        def _():
            to_left(b).start()

        @pl.when(near_right)
        def _():
            to_right(b).start()

        @pl.when(at_seam)
        def _():
            for p in (1, 3, 2, 0):
                seam_out(b, p).start()

    @pl.when(jnp.logical_not(has_left))
    def _():
        hal[:, :, BS:] = jnp.zeros((3, rows, BS), hal.dtype)
        tr_r[...] = jnp.zeros_like(tr_r)
        tail_r_in[...] = jnp.zeros_like(tail_r_in)
        mask_prev[...] = jnp.zeros_like(mask_prev)

    @pl.when(jnp.logical_not(has_right))
    def _():
        hal[:, :, :BS] = jnp.zeros((3, rows, BS), hal.dtype)
        tr_l[...] = jnp.zeros_like(tr_l)
        tail_l_in[...] = jnp.zeros_like(tail_l_in)

    acc[...] = jnp.zeros_like(acc)

    def inner_step(turned, wide, first):
        def step(c, carry):
            if first:
                load(c).wait()
            piece = pl.ds(pl.multiple_of(c * KC, KC), KC)
            for b in turned:
                xt[c, b * BS:(b + 1) * BS, :] = x[piece, b * BS:(b + 1) * BS].T
            for q in wide:
                lhs = xt[c, 0:INNER_M[q] * BS, :]
                rhs = x[piece, 2 * q * BS:(2 * q + 2) * BS]
                where = slice(INNER_OFF[q] * BS, (INNER_OFF[q] + INNER_M[q]) * BS)
                acc[where, :] += jnp.dot(lhs, rhs, preferred_element_type=jnp.float32)
            return carry

        lax.fori_loop(0, chunks, step, 0)

    def scaled(tile, keep):
        return (tile * (keep > 0).astype(jnp.float32)).astype(part.dtype)

    def put(tile, keep, t):
        part[:, t] = scaled(tile, keep).reshape(AUX, SL, BS)

    def put_inner(k):
        for u, (i, j) in enumerate(INNER_PART[k]):
            row = (INNER_OFF[j // 2] + i) * BS
            col = (j % 2) * BS
            put(acc[row:row + BS, col:col + BS], mask_own[i:i + 1, j - i - 1:j - i], T0[k] + u)

    def span_of(k):
        return pl.ds(T0[k], T0[k + 1] - T0[k])

    def send_far(k):
        return pltpu.make_async_remote_copy(
            part.at[AUX - 1 - pair, span_of(k)], far_sum.at[span_of(k)],
            fs.at[k], fr.at[k], device_id={"aux": pair}, device_id_type=MESH)

    def send_own(k):
        return pltpu.make_async_remote_copy(
            part.at[pair, span_of(k)], own_sum.at[span_of(k)],
            os.at[k], orr.at[k], device_id={"aux": pair}, device_id_type=MESH)

    def send_mirror(k):
        return pltpu.make_async_remote_copy(
            far_out.at[span_of(k)], far_in.at[span_of(k)],
            gs.at[k], gr.at[k], device_id={"aux": mirror}, device_id_type=MESH)

    def alpha(k):
        send_far(k).start()
        send_own(k).start()

    def beta(k):
        send_far(k).wait_recv()
        for t in range(T0[k], T0[k + 1]):
            far_out[t] = (part[mirror, t].astype(jnp.float32) + far_sum[t].astype(jnp.float32)).astype(part.dtype)
        send_mirror(k).start()

    def send_tail(r):
        return pltpu.make_async_remote_copy(
            part.at[aux_peer(r), pl.ds(TAIL, N_ALL - TAIL)], tail_in.at[r - 1],
            ds.at[r - 1], dr.at[r - 1], device_id={"aux": aux_peer(r)}, device_id_type=MESH)

    inner_step(range(0, 5), range(0, 3), True)
    put_inner(0)
    alpha(0)
    inner_step(range(5, NBLK), range(3, 4), False)
    put_inner(1)
    alpha(1)

    def cross(b):
        @pl.when(near_right)
        def _():
            to_left(b).wait_recv()

        @pl.when(near_left)
        def _():
            to_right(b).wait_recv()

        @pl.when(at_seam)
        def _():
            for p in range(AUX):
                seam_in(b, p).wait_recv()

        if b == 0:
            @pl.when(has_left)
            def _():
                mask_copy.wait_recv()

        lo, size = LO[b] * BS, (HI[b] - LO[b]) * BS
        acc[0:size, :] = jnp.zeros((size, 2 * BS), jnp.float32)

        def step(c, carry):
            piece = pl.ds(pl.multiple_of(c * KC, KC), KC)
            acc[0:size, :] += jnp.dot(
                xt[c, lo:lo + size, :], hal[b, piece, :], preferred_element_type=jnp.float32)
            return carry

        lax.fori_loop(0, chunks, step, 0)
        t = T0[b + 2]
        for u, (i, j) in enumerate(RIGHT[b]):
            own = NBLK - 1 - i
            row = (own - LO[b]) * BS
            tile = acc[row:row + BS, 0:BS]
            keep = mask_own[own:own + 1, i + j:i + j + 1]
            put(tile, keep, t)
            if b == 2:
                tail_r[:, u] = scaled(tile.T, keep).reshape(AUX, SL, BS)
            t += 1
        for u, (i, j) in enumerate(LEFT[b]):
            row = (j - LO[b]) * BS
            far = NBLK - 1 - i
            tile = acc[row:row + BS, BS:2 * BS]
            keep = mask_prev[far:far + 1, i + j:i + j + 1]
            put(tile, keep, t)
            if b == 2:
                tail_l[:, u] = scaled(tile.T, keep).reshape(AUX, SL, BS)
            t += 1

    def total(t):
        return part[a, t].astype(jnp.float32) + own_sum[t].astype(jnp.float32) + far_in[t].astype(jnp.float32)

    def turn(values, ts, g):
        values = values + [jnp.zeros((SL, BS), jnp.float32)] * (4 - len(values))
        ts[:, g] = jnp.concatenate(values, axis=0).T.astype(ts.dtype).reshape(AUX, SL, BS)

    def sums(t0, places, ts, g0):
        for g in range(groups_of(len(places))):
            values = []
            for u, (m, e) in enumerate(places[4 * g:4 * g + 4]):
                value = total(t0 + 4 * g + u)
                out_ref[m, e] = value
                values.append(value)
            turn(values, ts, g0 + g)

    def send_in(k, r):
        span = pl.ds(GI[k], GI[k + 1] - GI[k])
        return pltpu.make_async_remote_copy(
            ts_in.at[aux_peer(r), span], tr_in.at[a, span], s2s.at[k, r - 1], s2r.at[k, r - 1],
            device_id={"aux": aux_peer(r)}, device_id_type=MESH)

    def send_r(b, to):
        span = pl.ds(GR[b], GR[b + 1] - GR[b])
        return pltpu.make_async_remote_copy(
            ts_r.at[to, span], tr_r.at[a, span], crs.at[b, to], crr.at[b, a],
            device_id={"ao": right, "aux": to}, device_id_type=MESH)

    def send_l(b, to):
        span = pl.ds(GL[b], GL[b + 1] - GL[b])
        return pltpu.make_async_remote_copy(
            ts_l.at[to, span], tr_l.at[a, span], cls.at[b, to], clr.at[b, a],
            device_id={"ao": left, "aux": to}, device_id_type=MESH)

    def got_r(b, source):
        span = pl.ds(GR[b], GR[b + 1] - GR[b])
        return pltpu.make_async_remote_copy(
            ts_r.at[source, span], tr_r.at[source, span], crs.at[b, source], crr.at[b, source],
            device_id={"ao": left, "aux": source}, device_id_type=MESH)

    def got_l(b, source):
        span = pl.ds(GL[b], GL[b + 1] - GL[b])
        return pltpu.make_async_remote_copy(
            ts_l.at[source, span], tr_l.at[source, span], cls.at[b, source], clr.at[b, source],
            device_id={"ao": right, "aux": source}, device_id_type=MESH)

    def inner_sums(k):
        send_own(k).wait_recv()
        send_mirror(k).wait_recv()
        sums(T0[k], [(i, W + j - i - 1) for i, j in INNER_PART[k]], ts_in, GI[k])
        tr_in[a, GI[k]:GI[k + 1]] = ts_in[a, GI[k]:GI[k + 1]]
        for r in range(1, AUX):
            send_in(k, r).start()

    def cross_sums(b):
        send_own(b + 2).wait_recv()
        send_mirror(b + 2).wait_recv()
        t = T0[b + 2]
        sums(t, [(NBLK - 1 - i, W + i + j) for i, j in RIGHT[b]], ts_r, GR[b])

        @pl.when(has_right)
        def _():
            for to in range(AUX):
                send_r(b, to).start()

        sums(t + len(RIGHT[b]), [(j, W - 1 - i - j) for i, j in LEFT[b]], ts_l, GL[b])

        @pl.when(has_left)
        def _():
            for to in range(AUX):
                send_l(b, to).start()

    def place(tr, g0, places):
        for u, (m, e) in enumerate(places):
            g, v = g0 + u // 4, u % 4
            pieces = [tr[source, g, :, v * SL:(v + 1) * SL].astype(jnp.float32) for source in range(AUX)]
            out_ref[m, e] = jnp.concatenate(pieces, axis=1)

    def inner_place(k):
        for r in range(1, AUX):
            send_in(k, r).wait_recv()
        place(tr_in, GI[k], [(j, W - (j - i)) for i, j in INNER_PART[k]])

    def cross_place(b):
        @pl.when(has_left)
        def _():
            for source in range(AUX):
                got_r(b, source).wait_recv()

        place(tr_r, GR[b], [(j, W - 1 - i - j) for i, j in RIGHT[b]])

        @pl.when(has_right)
        def _():
            for source in range(AUX):
                got_l(b, source).wait_recv()

        place(tr_l, GL[b], [(NBLK - 1 - i, W + i + j) for i, j in LEFT[b]])

    def tail_to_right(to):
        return pltpu.make_async_remote_copy(
            tail_r.at[to], tail_r_in.at[a], crs.at[2, to], crr.at[2, a],
            device_id={"ao": right, "aux": to}, device_id_type=MESH)

    def tail_to_left(to):
        return pltpu.make_async_remote_copy(
            tail_l.at[to], tail_l_in.at[a], cls.at[2, to], clr.at[2, a],
            device_id={"ao": left, "aux": to}, device_id_type=MESH)

    def tail_from_left(source):
        return pltpu.make_async_remote_copy(
            tail_r.at[source], tail_r_in.at[source], crs.at[2, source], crr.at[2, source],
            device_id={"ao": left, "aux": source}, device_id_type=MESH)

    def tail_from_right(source):
        return pltpu.make_async_remote_copy(
            tail_l.at[source], tail_l_in.at[source], cls.at[2, source], clr.at[2, source],
            device_id={"ao": right, "aux": source}, device_id_type=MESH)

    def tail_send():
        for r in range(1, AUX):
            send_tail(r).start()

        @pl.when(has_right)
        def _():
            for to in range(AUX):
                tail_to_right(to).start()

        @pl.when(has_left)
        def _():
            for to in range(AUX):
                tail_to_left(to).start()

    def tail_finish():
        for r in range(1, AUX):
            send_tail(r).wait_recv()
        places = [(NBLK - 1 - i, W + i + j) for i, j in RIGHT[2]] + [(j, W - 1 - i - j) for i, j in LEFT[2]]
        for u, (m, e) in enumerate(places):
            value = part[a, TAIL + u].astype(jnp.float32)
            for r in range(1, AUX):
                value = value + tail_in[r - 1, u].astype(jnp.float32)
            out_ref[m, e] = value

        @pl.when(has_left)
        def _():
            for source in range(AUX):
                tail_from_left(source).wait_recv()

        @pl.when(has_right)
        def _():
            for source in range(AUX):
                tail_from_right(source).wait_recv()

        for u, (i, j) in enumerate(RIGHT[2]):
            value = tail_r_in[0, u].astype(jnp.float32)
            for source in range(1, AUX):
                value = value + tail_r_in[source, u].astype(jnp.float32)
            out_ref[j, W - 1 - i - j] = value
        for u, (i, j) in enumerate(LEFT[2]):
            value = tail_l_in[0, u].astype(jnp.float32)
            for source in range(1, AUX):
                value = value + tail_l_in[source, u].astype(jnp.float32)
            out_ref[NBLK - 1 - i, W + i + j] = value

    relay(0)
    beta(0)
    relay(1)
    cross(0)
    alpha(2)
    relay(2)
    beta(1)
    beta(2)
    inner_sums(0)
    inner_sums(1)
    cross(1)
    alpha(3)
    cross_sums(0)
    inner_place(0)
    inner_place(1)
    beta(3)
    cross(2)
    tail_send()
    cross_sums(1)
    cross_place(0)
    cross_place(1)
    tail_finish()

    for k in range(4):
        send_far(k).wait_send()
        send_own(k).wait_send()
        send_mirror(k).wait_send()
    for r in range(1, AUX):
        send_tail(r).wait_send()
        for k in range(2):
            send_in(k, r).wait_send()

    @pl.when(has_right)
    def _():
        mask_copy.wait_send()
        for to in range(AUX):
            tail_to_right(to).wait_send()
            for b in range(2):
                send_r(b, to).wait_send()

    @pl.when(has_left)
    def _():
        for to in range(AUX):
            tail_to_left(to).wait_send()
            for b in range(2):
                send_l(b, to).wait_send()

    for b in range(3):
        @pl.when(near_right)
        def _():
            to_right(b).wait_send()

        @pl.when(near_left)
        def _():
            to_left(b).wait_send()

        @pl.when(at_seam)
        def _():
            for p in range(AUX):
                seam_out(b, p).wait_send()

        for p in range(1, AUX):
            @pl.when(is_relay(p))
            def _():
                relay_out(b, p).wait_send()


def body(half_transformed, pair_mask):
    flat = half_transformed.reshape(-1, NBLK * BS)
    rows = flat.shape[0]
    bf16 = jnp.bfloat16
    dma = pltpu.SemaphoreType.DMA
    return pl.pallas_call(
        kernel,
        out_shape=jax.ShapeDtypeStruct((NBLK, 2 * W, SL, BS), jnp.float32),
        in_specs=[pl.BlockSpec(memory_space=pl.ANY), pl.BlockSpec(memory_space=pltpu.VMEM)],
        out_specs=pl.BlockSpec(memory_space=pltpu.VMEM),
        scratch_shapes=[
            pltpu.VMEM((rows, NBLK * BS), bf16),
            pltpu.VMEM((rows // KC, NBLK * BS, KC), bf16),
            pltpu.VMEM((3, rows, 2 * BS), bf16),
            pltpu.VMEM((3, rows // AUX, BS), bf16),
            pltpu.VMEM((sum(INNER_M) * BS, 2 * BS), jnp.float32),
            pltpu.VMEM((AUX, N_ALL, SL, BS), bf16),
            pltpu.VMEM((TAIL, SL, BS), bf16),
            pltpu.VMEM((TAIL, SL, BS), bf16),
            pltpu.VMEM((TAIL, SL, BS), bf16),
            pltpu.VMEM((TAIL, SL, BS), bf16),
            pltpu.VMEM((AUX - 1, N_ALL - TAIL, SL, BS), bf16),
            pltpu.VMEM((AUX, GI[2], SL, BS), bf16),
            pltpu.VMEM((AUX, GR[2], SL, BS), bf16),
            pltpu.VMEM((AUX, GL[2], SL, BS), bf16),
            pltpu.VMEM((AUX, GI[2], SL, BS), bf16),
            pltpu.VMEM((AUX, GR[2], SL, BS), bf16),
            pltpu.VMEM((AUX, GL[2], SL, BS), bf16),
            pltpu.VMEM((AUX, len(RIGHT[2]), SL, BS), bf16),
            pltpu.VMEM((AUX, len(LEFT[2]), SL, BS), bf16),
            pltpu.VMEM((AUX, len(RIGHT[2]), SL, BS), bf16),
            pltpu.VMEM((AUX, len(LEFT[2]), SL, BS), bf16),
            pltpu.VMEM((NBLK, BS), jnp.int32),
            pltpu.VMEM((NBLK, BS), jnp.int32),
            dma((rows // KC,)),
            dma((2, 3)), dma((2, 3)),
            dma((AUX, 3)), dma((AUX, 3)), dma((3,)), dma((3,)),
            dma, dma,
            dma((4,)), dma((4,)),
            dma((4,)), dma((4,)),
            dma((4,)), dma((4,)),
            dma((AUX - 1,)), dma((AUX - 1,)),
            dma((2, AUX - 1)), dma((2, AUX - 1)),
            dma((3, AUX)), dma((3, AUX)),
            dma((3, AUX)), dma((3, AUX)),
        ],
        compiler_params=pltpu.CompilerParams(
            collective_id=0, has_side_effects=True, vmem_limit_bytes=48 << 20),
        cost_estimate=pl.CostEstimate(flops=8 << 30, bytes_accessed=16 << 20, transcendentals=0),
    )(flat, pair_mask)


def solution(mesh):
    return jax.shard_map(
        body,
        mesh=mesh,
        in_specs=(P("aux", None, "ao"), P("ao", None)),
        out_specs=P("ao", None, "aux", None),
        check_vma=False,
    )
```

```python
import functools

import jax
import jax.numpy as jnp
from jax import lax
from jax.experimental import pallas as pl
from jax.experimental.pallas import tpu as pltpu
from jax.sharding import PartitionSpec as P

MESH = pl.DeviceIdType.MESH
BS = 128
W = 6
NBLK = 8
AUX = 4
SL = BS // AUX
KC = 1024
SEAM = 31
RELAY = [7, 15, 23, 0]
CUTS = [0, 512, 1536, 2560, 3584, 4096]
PATHS = len(RELAY) + 1

INNER = [(i, j) for j in range(1, NBLK) for i in range(max(0, j - W), j)]
INNER_M = [1, 3, 5, 7]
INNER_OFF = [0, 1, 4, 9]
RIGHT = [[(i, b) for i in range(b, W - b)] for b in range(3)]
LEFT = [[(b, j) for j in range(b + 1, W - b)] for b in range(3)]
LO = [1, 2, 3]
HI = [8, 7, 6]


def groups_of(count):
    return (count + 3) // 4


EARLY = 15
INNER_PART = [INNER[:EARLY], INNER[EARLY:]]
T0 = [0, EARLY, len(INNER)]
for b in range(3):
    T0.append(T0[-1] + len(RIGHT[b]) + len(LEFT[b]))
N_ALL = T0[-1]
TAIL = T0[4]
GI = [0, groups_of(EARLY), groups_of(EARLY) + groups_of(len(INNER) - EARLY)]
GR = [0]
GL = [0]
for b in range(2):
    GR.append(GR[-1] + groups_of(len(RIGHT[b])))
    GL.append(GL[-1] + groups_of(len(LEFT[b])))


def kernel(
    x_hbm, mask_ref, out_ref,
    x, xt, hal, rel, acc, part, own_sum, far_sum, far_out, far_in, tail_in,
    ts_in, ts_r, ts_l, tr_in, tr_r, tr_l, tail_r, tail_l, tail_r_in, tail_l_in, mask_own, mask_prev,
    load_sem, hs, hr, ss, sr, rs, rr, ms, mr,
    os, orr, fs, fr, gs, gr, ds, dr, s2s, s2r, crs, crr, cls, clr,
):
    rows = x.shape[0]
    chunks = rows // KC
    n = lax.axis_index("ao")
    a = lax.axis_index("aux")
    n_ao = lax.axis_size("ao")
    fwd = n <= SEAM
    at_seam = (n == SEAM) | (n == SEAM + 1)
    last = n_ao - 1
    has_left = n > 0
    has_right = n < n_ao - 1
    pair = a + 1 - 2 * lax.rem(a, 2)
    outer = (a == 0) | (a == AUX - 1)
    other_half = jnp.where(a < 2, 2, 0)
    left = jnp.maximum(n - 1, 0)
    right = jnp.minimum(n + 1, n_ao - 1)

    def aux_peer(r):
        return lax.rem(a + r, AUX)

    barrier = pltpu.get_barrier_semaphore()
    for r in range(1, AUX):
        pl.semaphore_signal(barrier, 1, device_id={"aux": aux_peer(r)}, device_id_type=MESH)

    @pl.when(has_left)
    def _():
        for b in range(AUX):
            pl.semaphore_signal(barrier, 1, device_id={"ao": left, "aux": b}, device_id_type=MESH)

    @pl.when(has_right)
    def _():
        for b in range(AUX):
            pl.semaphore_signal(barrier, 1, device_id={"ao": right, "aux": b}, device_id_type=MESH)

    def relay_of(p):
        return jnp.where(fwd, RELAY[p - 1], last - RELAY[p - 1])

    def is_relay(p):
        return n == relay_of(p)

    relay_to = jnp.where(fwd, SEAM + 1, SEAM)
    relay_from = jnp.where(fwd, SEAM, SEAM + 1)
    extra = jnp.where(at_seam, PATHS - 1, 0)
    for p in range(1, PATHS):
        extra += jnp.where(is_relay(p), 1, 0)

        @pl.when(is_relay(p))
        def _():
            pl.semaphore_signal(barrier, 1, device_id={"ao": relay_from}, device_id_type=MESH)

        @pl.when(at_seam)
        def _():
            other = jnp.where(fwd, last - RELAY[p - 1], RELAY[p - 1])
            pl.semaphore_signal(barrier, 1, device_id={"ao": other}, device_id_type=MESH)

    def load(c):
        piece = pl.ds(pl.multiple_of(c * KC, KC), KC)
        return pltpu.make_async_copy(x_hbm.at[piece], x.at[piece], load_sem.at[c])

    for c in range(chunks):
        load(c).start()
    mask_own[...] = jnp.zeros_like(mask_own)
    mask_own[:, 0:W] = mask_ref[...]

    pl.semaphore_wait(
        barrier, AUX - 1 + AUX * (has_left.astype(jnp.int32) + has_right.astype(jnp.int32)) + extra)

    def to_left(b):
        return pltpu.make_async_remote_copy(
            x_hbm.at[:, pl.ds(b * BS, BS)], hal.at[b, :, pl.ds(0, BS)],
            hs.at[0, b], hr.at[0, b], device_id={"ao": left}, device_id_type=MESH)

    def to_right(b):
        return pltpu.make_async_remote_copy(
            x_hbm.at[:, pl.ds((NBLK - 1 - b) * BS, BS)], hal.at[b, :, pl.ds(BS, BS)],
            hs.at[1, b], hr.at[1, b], device_id={"ao": right}, device_id_type=MESH)

    def seam_span(p, lanes):
        return (pl.ds(CUTS[p], CUTS[p + 1] - CUTS[p]), pl.ds(pl.multiple_of(lanes, BS), BS))

    def parked(b, p):
        return rel.at[b, pl.ds(0, CUTS[p + 1] - CUTS[p])]

    def seam_out(b, p):
        source = x_hbm.at[seam_span(p, jnp.where(fwd, (NBLK - 1 - b) * BS, b * BS))]
        if p == 0:
            return pltpu.make_async_remote_copy(
                source, hal.at[(b,) + seam_span(p, jnp.where(fwd, BS, 0))],
                ss.at[p, b], sr.at[p, b], device_id={"ao": relay_to}, device_id_type=MESH)
        return pltpu.make_async_remote_copy(
            source, parked(b, p), ss.at[p, b], rr.at[b], device_id={"ao": relay_of(p)}, device_id_type=MESH)

    def relay_out(b, p):
        return pltpu.make_async_remote_copy(
            parked(b, p), hal.at[(b,) + seam_span(p, jnp.where(fwd, BS, 0))],
            rs.at[b], sr.at[p, b], device_id={"ao": relay_to}, device_id_type=MESH)

    def seam_in(b, p):
        return pltpu.make_async_remote_copy(
            parked(b, p), hal.at[(b,) + seam_span(p, jnp.where(fwd, 0, BS))],
            rs.at[b], sr.at[p, b], device_id={"ao": relay_to}, device_id_type=MESH)

    def relay(b):
        for p in range(1, PATHS):
            @pl.when(is_relay(p))
            def _():
                seam_out(b, p).wait_recv()
                relay_out(b, p).start()

    near_left = has_left & (n != SEAM + 1)
    near_right = has_right & (n != SEAM)
    mask_copy = pltpu.make_async_remote_copy(
        mask_own, mask_prev, ms, mr, device_id={"ao": right}, device_id_type=MESH)

    @pl.when(has_right)
    def _():
        mask_copy.start()

    for b in range(3):
        @pl.when(near_left)
        def _():
            to_left(b).start()

        @pl.when(near_right)
        def _():
            to_right(b).start()

        @pl.when(at_seam)
        def _():
            for p in (1, 2, 4, 3, 0):
                seam_out(b, p).start()

    @pl.when(jnp.logical_not(has_left))
    def _():
        hal[:, :, BS:] = jnp.zeros((3, rows, BS), hal.dtype)
        tr_r[...] = jnp.zeros_like(tr_r)
        tail_r_in[...] = jnp.zeros_like(tail_r_in)
        mask_prev[...] = jnp.zeros_like(mask_prev)

    @pl.when(jnp.logical_not(has_right))
    def _():
        hal[:, :, :BS] = jnp.zeros((3, rows, BS), hal.dtype)
        tr_l[...] = jnp.zeros_like(tr_l)
        tail_l_in[...] = jnp.zeros_like(tail_l_in)

    acc[...] = jnp.zeros_like(acc)

    def inner_step(turned, wide, first):
        def step(c, carry):
            if first:
                load(c).wait()
            piece = pl.ds(pl.multiple_of(c * KC, KC), KC)
            for b in turned:
                xt[c, b * BS:(b + 1) * BS, :] = x[piece, b * BS:(b + 1) * BS].T
            for q in wide:
                lhs = xt[c, 0:INNER_M[q] * BS, :]
                rhs = x[piece, 2 * q * BS:(2 * q + 2) * BS]
                where = slice(INNER_OFF[q] * BS, (INNER_OFF[q] + INNER_M[q]) * BS)
                acc[where, :] += jnp.dot(lhs, rhs, preferred_element_type=jnp.float32)
            return carry

        lax.fori_loop(0, chunks, step, 0)

    def scaled(tile, keep):
        return (tile * (keep > 0).astype(jnp.float32)).astype(part.dtype)

    def put(tile, keep, t):
        part[:, t] = scaled(tile, keep).reshape(AUX, SL, BS)

    def put_inner(k):
        for u, (i, j) in enumerate(INNER_PART[k]):
            row = (INNER_OFF[j // 2] + i) * BS
            col = (j % 2) * BS
            put(acc[row:row + BS, col:col + BS], mask_own[i:i + 1, j - i - 1:j - i], T0[k] + u)

    def span_of(k):
        return pl.ds(T0[k], T0[k + 1] - T0[k])

    def send_far(k):
        return pltpu.make_async_remote_copy(
            part.at[pl.ds(other_half, 2), span_of(k)], far_sum.at[:, span_of(k)],
            fs.at[k], fr.at[k], device_id={"aux": pair}, device_id_type=MESH)

    def send_own(k):
        return pltpu.make_async_remote_copy(
            part.at[pair, span_of(k)], own_sum.at[span_of(k)],
            os.at[k], orr.at[k], device_id={"aux": pair}, device_id_type=MESH)

    def send_joined(k, h):
        return pltpu.make_async_remote_copy(
            far_out.at[h, span_of(k)], far_in.at[span_of(k)],
            gs.at[k, h], gr.at[k], device_id={"aux": other_half + h}, device_id_type=MESH)

    def alpha(k):
        @pl.when(outer)
        def _():
            send_far(k).start()

        send_own(k).start()

    def beta(k):
        @pl.when(jnp.logical_not(outer))
        def _():
            send_far(k).wait_recv()
            for h in range(2):
                for t in range(T0[k], T0[k + 1]):
                    far_out[h, t] = (
                        part[other_half + h, t].astype(jnp.float32) + far_sum[h, t].astype(jnp.float32)
                    ).astype(part.dtype)
                send_joined(k, h).start()

    def send_tail(r):
        return pltpu.make_async_remote_copy(
            part.at[aux_peer(r), pl.ds(TAIL, N_ALL - TAIL)], tail_in.at[r - 1],
            ds.at[r - 1], dr.at[r - 1], device_id={"aux": aux_peer(r)}, device_id_type=MESH)

    inner_step(range(0, 5), range(0, 3), True)
    put_inner(0)
    alpha(0)
    relay(0)
    inner_step(range(5, NBLK), range(3, 4), False)
    put_inner(1)
    alpha(1)

    def cross(b):
        @pl.when(near_right)
        def _():
            to_left(b).wait_recv()

        @pl.when(near_left)
        def _():
            to_right(b).wait_recv()

        @pl.when(at_seam)
        def _():
            for p in range(PATHS):
                seam_in(b, p).wait_recv()

        if b == 0:
            @pl.when(has_left)
            def _():
                mask_copy.wait_recv()

        lo, size = LO[b] * BS, (HI[b] - LO[b]) * BS
        acc[0:size, :] = jnp.zeros((size, 2 * BS), jnp.float32)

        def step(c, carry):
            piece = pl.ds(pl.multiple_of(c * KC, KC), KC)
            acc[0:size, :] += jnp.dot(
                xt[c, lo:lo + size, :], hal[b, piece, :], preferred_element_type=jnp.float32)
            return carry

        lax.fori_loop(0, chunks, step, 0)
        t = T0[b + 2]
        for u, (i, j) in enumerate(RIGHT[b]):
            own = NBLK - 1 - i
            row = (own - LO[b]) * BS
            tile = acc[row:row + BS, 0:BS]
            keep = mask_own[own:own + 1, i + j:i + j + 1]
            put(tile, keep, t)
            if b == 2:
                tail_r[:, u] = scaled(tile.T, keep).reshape(AUX, SL, BS)
            t += 1
        for u, (i, j) in enumerate(LEFT[b]):
            row = (j - LO[b]) * BS
            far = NBLK - 1 - i
            tile = acc[row:row + BS, BS:2 * BS]
            keep = mask_prev[far:far + 1, i + j:i + j + 1]
            put(tile, keep, t)
            if b == 2:
                tail_l[:, u] = scaled(tile.T, keep).reshape(AUX, SL, BS)
            t += 1

    def total(t):
        return part[a, t].astype(jnp.float32) + own_sum[t].astype(jnp.float32) + far_in[t].astype(jnp.float32)

    def turn(values, ts, g):
        values = values + [jnp.zeros((SL, BS), jnp.float32)] * (4 - len(values))
        ts[:, g] = jnp.concatenate(values, axis=0).T.astype(ts.dtype).reshape(AUX, SL, BS)

    def sums(t0, places, ts, g0):
        for g in range(groups_of(len(places))):
            values = []
            for u, (m, e) in enumerate(places[4 * g:4 * g + 4]):
                value = total(t0 + 4 * g + u)
                out_ref[m, e] = value
                values.append(value)
            turn(values, ts, g0 + g)

    def send_in(k, r):
        span = pl.ds(GI[k], GI[k + 1] - GI[k])
        return pltpu.make_async_remote_copy(
            ts_in.at[aux_peer(r), span], tr_in.at[a, span], s2s.at[k, r - 1], s2r.at[k, r - 1],
            device_id={"aux": aux_peer(r)}, device_id_type=MESH)

    def send_r(b, to):
        span = pl.ds(GR[b], GR[b + 1] - GR[b])
        return pltpu.make_async_remote_copy(
            ts_r.at[to, span], tr_r.at[a, span], crs.at[b, to], crr.at[b, a],
            device_id={"ao": right, "aux": to}, device_id_type=MESH)

    def send_l(b, to):
        span = pl.ds(GL[b], GL[b + 1] - GL[b])
        return pltpu.make_async_remote_copy(
            ts_l.at[to, span], tr_l.at[a, span], cls.at[b, to], clr.at[b, a],
            device_id={"ao": left, "aux": to}, device_id_type=MESH)

    def got_r(b, source):
        span = pl.ds(GR[b], GR[b + 1] - GR[b])
        return pltpu.make_async_remote_copy(
            ts_r.at[source, span], tr_r.at[source, span], crs.at[b, source], crr.at[b, source],
            device_id={"ao": left, "aux": source}, device_id_type=MESH)

    def got_l(b, source):
        span = pl.ds(GL[b], GL[b + 1] - GL[b])
        return pltpu.make_async_remote_copy(
            ts_l.at[source, span], tr_l.at[source, span], cls.at[b, source], clr.at[b, source],
            device_id={"ao": right, "aux": source}, device_id_type=MESH)

    def inner_sums(k):
        send_own(k).wait_recv()
        send_joined(k, 0).wait_recv()
        sums(T0[k], [(i, W + j - i - 1) for i, j in INNER_PART[k]], ts_in, GI[k])
        tr_in[a, GI[k]:GI[k + 1]] = ts_in[a, GI[k]:GI[k + 1]]
        for r in range(1, AUX):
            send_in(k, r).start()

    def cross_sums(b):
        send_own(b + 2).wait_recv()
        send_joined(b + 2, 0).wait_recv()
        t = T0[b + 2]
        sums(t, [(NBLK - 1 - i, W + i + j) for i, j in RIGHT[b]], ts_r, GR[b])

        @pl.when(has_right)
        def _():
            for to in range(AUX):
                send_r(b, to).start()

        sums(t + len(RIGHT[b]), [(j, W - 1 - i - j) for i, j in LEFT[b]], ts_l, GL[b])

        @pl.when(has_left)
        def _():
            for to in range(AUX):
                send_l(b, to).start()

    def place(tr, g0, places):
        for u, (m, e) in enumerate(places):
            g, v = g0 + u // 4, u % 4
            pieces = [tr[source, g, :, v * SL:(v + 1) * SL].astype(jnp.float32) for source in range(AUX)]
            out_ref[m, e] = jnp.concatenate(pieces, axis=1)

    def inner_place(k):
        for r in range(1, AUX):
            send_in(k, r).wait_recv()
        place(tr_in, GI[k], [(j, W - (j - i)) for i, j in INNER_PART[k]])

    def cross_place(b):
        @pl.when(has_left)
        def _():
            for source in range(AUX):
                got_r(b, source).wait_recv()

        place(tr_r, GR[b], [(j, W - 1 - i - j) for i, j in RIGHT[b]])

        @pl.when(has_right)
        def _():
            for source in range(AUX):
                got_l(b, source).wait_recv()

        place(tr_l, GL[b], [(NBLK - 1 - i, W + i + j) for i, j in LEFT[b]])

    def tail_to_right(to):
        return pltpu.make_async_remote_copy(
            tail_r.at[to], tail_r_in.at[a], crs.at[2, to], crr.at[2, a],
            device_id={"ao": right, "aux": to}, device_id_type=MESH)

    def tail_to_left(to):
        return pltpu.make_async_remote_copy(
            tail_l.at[to], tail_l_in.at[a], cls.at[2, to], clr.at[2, a],
            device_id={"ao": left, "aux": to}, device_id_type=MESH)

    def tail_from_left(source):
        return pltpu.make_async_remote_copy(
            tail_r.at[source], tail_r_in.at[source], crs.at[2, source], crr.at[2, source],
            device_id={"ao": left, "aux": source}, device_id_type=MESH)

    def tail_from_right(source):
        return pltpu.make_async_remote_copy(
            tail_l.at[source], tail_l_in.at[source], cls.at[2, source], clr.at[2, source],
            device_id={"ao": right, "aux": source}, device_id_type=MESH)

    def tail_send():
        for r in range(1, AUX):
            send_tail(r).start()

        @pl.when(has_right)
        def _():
            for to in range(AUX):
                tail_to_right(to).start()

        @pl.when(has_left)
        def _():
            for to in range(AUX):
                tail_to_left(to).start()

    def tail_finish():
        for r in range(1, AUX):
            send_tail(r).wait_recv()
        places = [(NBLK - 1 - i, W + i + j) for i, j in RIGHT[2]] + [(j, W - 1 - i - j) for i, j in LEFT[2]]
        for u, (m, e) in enumerate(places):
            value = part[a, TAIL + u].astype(jnp.float32)
            for r in range(1, AUX):
                value = value + tail_in[r - 1, u].astype(jnp.float32)
            out_ref[m, e] = value

        @pl.when(has_left)
        def _():
            for source in range(AUX):
                tail_from_left(source).wait_recv()

        @pl.when(has_right)
        def _():
            for source in range(AUX):
                tail_from_right(source).wait_recv()

        for u, (i, j) in enumerate(RIGHT[2]):
            value = tail_r_in[0, u].astype(jnp.float32)
            for source in range(1, AUX):
                value = value + tail_r_in[source, u].astype(jnp.float32)
            out_ref[j, W - 1 - i - j] = value
        for u, (i, j) in enumerate(LEFT[2]):
            value = tail_l_in[0, u].astype(jnp.float32)
            for source in range(1, AUX):
                value = value + tail_l_in[source, u].astype(jnp.float32)
            out_ref[NBLK - 1 - i, W + i + j] = value

    beta(0)
    relay(1)
    cross(0)
    alpha(2)
    relay(2)
    beta(1)
    beta(2)
    inner_sums(0)
    inner_sums(1)
    cross(1)
    alpha(3)
    cross_sums(0)
    inner_place(0)
    inner_place(1)
    beta(3)
    cross(2)
    tail_send()
    cross_sums(1)
    cross_place(0)
    cross_place(1)
    tail_finish()

    for k in range(4):
        send_own(k).wait_send()

        @pl.when(outer)
        def _():
            send_far(k).wait_send()

        @pl.when(jnp.logical_not(outer))
        def _():
            for h in range(2):
                send_joined(k, h).wait_send()

    for r in range(1, AUX):
        send_tail(r).wait_send()
        for k in range(2):
            send_in(k, r).wait_send()

    @pl.when(has_right)
    def _():
        mask_copy.wait_send()
        for to in range(AUX):
            tail_to_right(to).wait_send()
            for b in range(2):
                send_r(b, to).wait_send()

    @pl.when(has_left)
    def _():
        for to in range(AUX):
            tail_to_left(to).wait_send()
            for b in range(2):
                send_l(b, to).wait_send()

    for b in range(3):
        @pl.when(near_right)
        def _():
            to_right(b).wait_send()

        @pl.when(near_left)
        def _():
            to_left(b).wait_send()

        @pl.when(at_seam)
        def _():
            for p in range(PATHS):
                seam_out(b, p).wait_send()

        for p in range(1, PATHS):
            @pl.when(is_relay(p))
            def _():
                relay_out(b, p).wait_send()


def body(half_transformed, pair_mask):
    flat = half_transformed.reshape(-1, NBLK * BS)
    rows = flat.shape[0]
    bf16 = jnp.bfloat16
    dma = pltpu.SemaphoreType.DMA
    return pl.pallas_call(
        kernel,
        out_shape=jax.ShapeDtypeStruct((NBLK, 2 * W, SL, BS), jnp.float32),
        in_specs=[pl.BlockSpec(memory_space=pl.ANY), pl.BlockSpec(memory_space=pltpu.VMEM)],
        out_specs=pl.BlockSpec(memory_space=pltpu.VMEM),
        scratch_shapes=[
            pltpu.VMEM((rows, NBLK * BS), bf16),
            pltpu.VMEM((rows // KC, NBLK * BS, KC), bf16),
            pltpu.VMEM((3, rows, 2 * BS), bf16),
            pltpu.VMEM((3, max(CUTS[p + 1] - CUTS[p] for p in range(1, PATHS)), BS), bf16),
            pltpu.VMEM((sum(INNER_M) * BS, 2 * BS), jnp.float32),
            pltpu.VMEM((AUX, N_ALL, SL, BS), bf16),
            pltpu.VMEM((TAIL, SL, BS), bf16),
            pltpu.VMEM((2, TAIL, SL, BS), bf16),
            pltpu.VMEM((2, TAIL, SL, BS), bf16),
            pltpu.VMEM((TAIL, SL, BS), bf16),
            pltpu.VMEM((AUX - 1, N_ALL - TAIL, SL, BS), bf16),
            pltpu.VMEM((AUX, GI[2], SL, BS), bf16),
            pltpu.VMEM((AUX, GR[2], SL, BS), bf16),
            pltpu.VMEM((AUX, GL[2], SL, BS), bf16),
            pltpu.VMEM((AUX, GI[2], SL, BS), bf16),
            pltpu.VMEM((AUX, GR[2], SL, BS), bf16),
            pltpu.VMEM((AUX, GL[2], SL, BS), bf16),
            pltpu.VMEM((AUX, len(RIGHT[2]), SL, BS), bf16),
            pltpu.VMEM((AUX, len(LEFT[2]), SL, BS), bf16),
            pltpu.VMEM((AUX, len(RIGHT[2]), SL, BS), bf16),
            pltpu.VMEM((AUX, len(LEFT[2]), SL, BS), bf16),
            pltpu.VMEM((NBLK, BS), jnp.int32),
            pltpu.VMEM((NBLK, BS), jnp.int32),
            dma((rows // KC,)),
            dma((2, 3)), dma((2, 3)),
            dma((PATHS, 3)), dma((PATHS, 3)), dma((3,)), dma((3,)),
            dma, dma,
            dma((4,)), dma((4,)),
            dma((4,)), dma((4,)),
            dma((4, 2)), dma((4,)),
            dma((AUX - 1,)), dma((AUX - 1,)),
            dma((2, AUX - 1)), dma((2, AUX - 1)),
            dma((3, AUX)), dma((3, AUX)),
            dma((3, AUX)), dma((3, AUX)),
        ],
        compiler_params=pltpu.CompilerParams(
            collective_id=0, has_side_effects=True, vmem_limit_bytes=48 << 20),
        cost_estimate=pl.CostEstimate(flops=8 << 30, bytes_accessed=16 << 20, transcendentals=0),
    )(flat, pair_mask)


def solution(mesh):
    return jax.shard_map(
        body,
        mesh=mesh,
        in_specs=(P("aux", None, "ao"), P("ao", None)),
        out_specs=P("ao", None, "aux", None),
        check_vma=False,
    )
```

```python
import functools

import jax
import jax.numpy as jnp
from jax import lax
from jax.experimental import pallas as pl
from jax.experimental.pallas import tpu as pltpu
from jax.sharding import PartitionSpec as P

MESH = pl.DeviceIdType.MESH
BS = 128
W = 6
NBLK = 8
AUX = 4
SL = BS // AUX
KC = 1024
SEAM = 31
RELAY = [6, 14, 22, 0]
CUTS = [0, 640, 1536, 2560, 3456, 4096]
PATHS = len(RELAY) + 1

INNER = [(i, j) for j in range(1, NBLK) for i in range(max(0, j - W), j)]
INNER_M = [1, 3, 5, 7]
INNER_OFF = [0, 1, 4, 9]
RIGHT = [[(i, b) for i in range(b, W - b)] for b in range(3)]
LEFT = [[(b, j) for j in range(b + 1, W - b)] for b in range(3)]
def groups_of(count):
    return (count + 3) // 4


EARLY = 15
INNER_PART = [INNER[:EARLY], INNER[EARLY:]]
FAST, SLOW0, SLOW1, LAST = 2, 3, 4, 5
GI = [0, groups_of(EARLY), groups_of(EARLY) + groups_of(len(INNER) - EARLY)]
SIDES = {"R": RIGHT, "L": LEFT}
BASE = {"R": len(INNER), "L": len(INNER) + sum(map(len, RIGHT))}
N_ALL = BASE["L"] + sum(map(len, LEFT))
GX = {FAST: (0, 3), SLOW0: (0, 2), SLOW1: (2, 3)}


def tiles_of(k, side):
    if k < FAST:
        return INNER_PART[k]
    if k == FAST:
        return sum(SIDES[side], [])
    return SIDES[side][k - SLOW0]


def start_of(k, side):
    if k < FAST:
        return k * EARLY
    if k == FAST:
        return BASE[side]
    return BASE[side] + sum(map(len, SIDES[side][:k - SLOW0]))


def rows_of(side, b):
    return (2 + b, NBLK - b) if side == "R" else (1 + b, W - b)


def kernel(
    x_hbm, mask_hbm, out_ref,
    x, xt, hal, rel, acc, part, own_sum, far_sum, far_out, far_in, tail_in,
    ts_in, ts_r, ts_l, tr_in, tr_r, tr_l, tail_r, tail_l, tail_r_in, tail_l_in, mask_own, mask_prev,
    load_sem, mask_sem, hs, hr, ss, sr, rs, rr, ms, mr,
    os, orr, fs, fr, gs, gr, ds, dr, s2s, s2r, cs, cr,
):
    rows = x.shape[0]
    chunks = rows // KC
    n = lax.axis_index("ao")
    a = lax.axis_index("aux")
    n_ao = lax.axis_size("ao")
    fwd = n <= SEAM
    at_seam = (n == SEAM) | (n == SEAM + 1)
    last = n_ao - 1
    even = lax.rem(n, 2) == 0
    has_left = n > 0
    has_right = n < n_ao - 1
    pair = a + 1 - 2 * lax.rem(a, 2)
    outer = (a == 0) | (a == AUX - 1)
    other_half = jnp.where(a < 2, 2, 0)
    left = jnp.maximum(n - 1, 0)
    right = jnp.minimum(n + 1, n_ao - 1)

    def aux_peer(r):
        return lax.rem(a + r, AUX)

    barrier = pltpu.get_barrier_semaphore()
    for r in range(1, AUX):
        pl.semaphore_signal(barrier, 1, device_id={"aux": aux_peer(r)}, device_id_type=MESH)

    @pl.when(has_left)
    def _():
        for b in range(AUX):
            pl.semaphore_signal(barrier, 1, device_id={"ao": left, "aux": b}, device_id_type=MESH)

    @pl.when(has_right)
    def _():
        for b in range(AUX):
            pl.semaphore_signal(barrier, 1, device_id={"ao": right, "aux": b}, device_id_type=MESH)

    def relay_of(p):
        return jnp.where(fwd, RELAY[p - 1], last - RELAY[p - 1])

    def is_relay(p):
        return n == relay_of(p)

    relay_to = jnp.where(fwd, SEAM + 1, SEAM)
    relay_from = jnp.where(fwd, SEAM, SEAM + 1)
    extra = jnp.where(at_seam, PATHS - 1, 0)
    for p in range(1, PATHS):
        extra += jnp.where(is_relay(p), 1, 0)

        @pl.when(is_relay(p))
        def _():
            pl.semaphore_signal(barrier, 1, device_id={"ao": relay_from}, device_id_type=MESH)

        @pl.when(at_seam)
        def _():
            other = jnp.where(fwd, last - RELAY[p - 1], RELAY[p - 1])
            pl.semaphore_signal(barrier, 1, device_id={"ao": other}, device_id_type=MESH)

    def load(c):
        piece = pl.ds(pl.multiple_of(c * KC, KC), KC)
        return pltpu.make_async_copy(x_hbm.at[piece], x.at[piece], load_sem.at[c])

    for c in range(chunks):
        load(c).start()
    mask_load = pltpu.make_async_copy(mask_hbm, mask_own, mask_sem)
    mask_load.start()

    pl.semaphore_wait(
        barrier, AUX - 1 + AUX * (has_left.astype(jnp.int32) + has_right.astype(jnp.int32)) + extra)

    def to_left(b):
        return pltpu.make_async_remote_copy(
            x_hbm.at[:, pl.ds(b * BS, BS)], hal.at[b, :, pl.ds(0, BS)],
            hs.at[0, b], hr.at[0, b], device_id={"ao": left}, device_id_type=MESH)

    def to_right(b):
        return pltpu.make_async_remote_copy(
            x_hbm.at[:, pl.ds((NBLK - 1 - b) * BS, BS)], hal.at[b, :, pl.ds(BS, BS)],
            hs.at[1, b], hr.at[1, b], device_id={"ao": right}, device_id_type=MESH)

    def seam_span(p, lanes):
        return (pl.ds(CUTS[p], CUTS[p + 1] - CUTS[p]), pl.ds(pl.multiple_of(lanes, BS), BS))

    def parked(b, p):
        return rel.at[b, pl.ds(0, CUTS[p + 1] - CUTS[p])]

    def seam_out(b, p):
        source = x_hbm.at[seam_span(p, jnp.where(fwd, (NBLK - 1 - b) * BS, b * BS))]
        if p == 0:
            return pltpu.make_async_remote_copy(
                source, hal.at[(b,) + seam_span(p, jnp.where(fwd, BS, 0))],
                ss.at[p, b], sr.at[p, b], device_id={"ao": relay_to}, device_id_type=MESH)
        return pltpu.make_async_remote_copy(
            source, parked(b, p), ss.at[p, b], rr.at[b], device_id={"ao": relay_of(p)}, device_id_type=MESH)

    def relay_out(b, p):
        return pltpu.make_async_remote_copy(
            parked(b, p), hal.at[(b,) + seam_span(p, jnp.where(fwd, BS, 0))],
            rs.at[b], sr.at[p, b], device_id={"ao": relay_to}, device_id_type=MESH)

    def seam_in(b, p):
        return pltpu.make_async_remote_copy(
            parked(b, p), hal.at[(b,) + seam_span(p, jnp.where(fwd, 0, BS))],
            rs.at[b], sr.at[p, b], device_id={"ao": relay_to}, device_id_type=MESH)

    def relay(b):
        for p in range(1, PATHS):
            @pl.when(is_relay(p))
            def _():
                seam_out(b, p).wait_recv()
                relay_out(b, p).start()

    near_left = has_left & (n != SEAM + 1)
    near_right = has_right & (n != SEAM)
    mask_copy = pltpu.make_async_remote_copy(
        mask_own, mask_prev, ms, mr, device_id={"ao": right}, device_id_type=MESH)

    mask_load.wait()

    @pl.when(has_right)
    def _():
        mask_copy.start()

    for b in range(3):
        @pl.when(near_left)
        def _():
            to_left(b).start()

        @pl.when(near_right)
        def _():
            to_right(b).start()

        @pl.when(at_seam)
        def _():
            for p in (1, 2, 4, 3, 0):
                seam_out(b, p).start()

    @pl.when(jnp.logical_not(has_left))
    def _():
        hal[:, :, BS:] = jnp.zeros((3, rows, BS), hal.dtype)
        tr_r[...] = jnp.zeros_like(tr_r)
        tail_r_in[...] = jnp.zeros_like(tail_r_in)
        mask_prev[...] = jnp.zeros_like(mask_prev)

    @pl.when(jnp.logical_not(has_right))
    def _():
        hal[:, :, :BS] = jnp.zeros((3, rows, BS), hal.dtype)
        tr_l[...] = jnp.zeros_like(tr_l)
        tail_l_in[...] = jnp.zeros_like(tail_l_in)

    acc[...] = jnp.zeros_like(acc)

    def inner_step(turned, wide, first):
        def step(c, carry):
            if first:
                load(c).wait()
            piece = pl.ds(pl.multiple_of(c * KC, KC), KC)
            for b in turned:
                xt[c, b * BS:(b + 1) * BS, :] = x[piece, b * BS:(b + 1) * BS].T
            for q in wide:
                lhs = xt[c, 0:INNER_M[q] * BS, :]
                rhs = x[piece, 2 * q * BS:(2 * q + 2) * BS]
                where = slice(INNER_OFF[q] * BS, (INNER_OFF[q] + INNER_M[q]) * BS)
                acc[where, :] += jnp.dot(lhs, rhs, preferred_element_type=jnp.float32)
            return carry

        lax.fori_loop(0, chunks, step, 0)

    def scaled(tile, keep):
        return (tile * (keep > 0).astype(jnp.float32)).astype(part.dtype)

    def put(tile, keep, t):
        part[:, t] = scaled(tile, keep).reshape(AUX, SL, BS)

    def put_inner(k):
        for u, (i, j) in enumerate(INNER_PART[k]):
            row = (INNER_OFF[j // 2] + i) * BS
            col = (j % 2) * BS
            put(acc[row:row + BS, col:col + BS], mask_own[i:i + 1, j - i - 1:j - i], k * EARLY + u)

    def span_of(k, side):
        return pl.ds(start_of(k, side), len(tiles_of(k, side)))

    def send_far(k, side):
        return pltpu.make_async_remote_copy(
            part.at[pl.ds(other_half, 2), span_of(k, side)], far_sum.at[:, span_of(k, side)],
            fs.at[k], fr.at[k], device_id={"aux": pair}, device_id_type=MESH)

    def send_own(k, side):
        return pltpu.make_async_remote_copy(
            part.at[pair, span_of(k, side)], own_sum.at[span_of(k, side)],
            os.at[k], orr.at[k], device_id={"aux": pair}, device_id_type=MESH)

    def send_joined(k, h, side):
        return pltpu.make_async_remote_copy(
            far_out.at[h, span_of(k, side)], far_in.at[span_of(k, side)],
            gs.at[k, h], gr.at[k], device_id={"aux": other_half + h}, device_id_type=MESH)

    def alpha(k, side):
        @pl.when(outer)
        def _():
            send_far(k, side).start()

        send_own(k, side).start()

    def beta(k, side):
        @pl.when(jnp.logical_not(outer))
        def _():
            send_far(k, side).wait_recv()
            for h in range(2):
                for t in range(start_of(k, side), start_of(k, side) + len(tiles_of(k, side))):
                    far_out[h, t] = (
                        part[other_half + h, t].astype(jnp.float32) + far_sum[h, t].astype(jnp.float32)
                    ).astype(part.dtype)
                send_joined(k, h, side).start()

    def send_tail(r, side):
        count = len(tiles_of(LAST, side))
        return pltpu.make_async_remote_copy(
            part.at[aux_peer(r), span_of(LAST, side)], tail_in.at[r - 1, pl.ds(0, count)],
            ds.at[r - 1], dr.at[r - 1], device_id={"aux": aux_peer(r)}, device_id_type=MESH)

    inner_step(range(0, 5), range(0, 3), True)
    put_inner(0)
    alpha(0, None)
    relay(0)
    inner_step(range(5, NBLK), range(3, 4), False)
    put_inner(1)
    alpha(1, None)

    def arrive(side, b):
        if side == "R":
            @pl.when(near_right)
            def _():
                to_left(b).wait_recv()
        else:
            @pl.when(near_left)
            def _():
                to_right(b).wait_recv()

            if b == 0:
                @pl.when(has_left)
                def _():
                    mask_copy.wait_recv()

    def cross(side, b, slow):
        arrive(side, b)
        if slow:
            @pl.when(at_seam)
            def _():
                for p in range(PATHS):
                    seam_in(b, p).wait_recv()

        lo, hi = rows_of(side, b)
        size = (hi - lo) * BS
        lanes = slice(0, BS) if side == "R" else slice(BS, 2 * BS)
        acc[0:size, 0:BS] = jnp.zeros((size, BS), jnp.float32)

        def step(c, carry):
            piece = pl.ds(pl.multiple_of(c * KC, KC), KC)
            acc[0:size, 0:BS] += jnp.dot(
                xt[c, lo * BS:hi * BS, :], hal[b, piece, lanes], preferred_element_type=jnp.float32)
            return carry

        lax.fori_loop(0, chunks, step, 0)
        t0 = start_of(SLOW0 + b, side)
        for u, (i, j) in enumerate(SIDES[side][b]):
            far = NBLK - 1 - i
            row = ((far if side == "R" else j) - lo) * BS
            tile = acc[row:row + BS, 0:BS]
            keep = (mask_own if side == "R" else mask_prev)[far:far + 1, i + j:i + j + 1]
            put(tile, keep, t0 + u)
            if slow and b == 2:
                (tail_r if side == "R" else tail_l)[:, u] = scaled(tile.T, keep).reshape(AUX, SL, BS)

    def total(t):
        return part[a, t].astype(jnp.float32) + own_sum[t].astype(jnp.float32) + far_in[t].astype(jnp.float32)

    def turn(values, ts, g):
        values = values + [jnp.zeros((SL, BS), jnp.float32)] * (4 - len(values))
        ts[:, g] = jnp.concatenate(values, axis=0).T.astype(ts.dtype).reshape(AUX, SL, BS)

    def sums(t0, places, ts, g0):
        for g in range(groups_of(len(places))):
            values = []
            for u, (m, e) in enumerate(places[4 * g:4 * g + 4]):
                value = total(t0 + 4 * g + u)
                out_ref[m, e] = value
                values.append(value)
            turn(values, ts, g0 + g)

    def send_in(k, r):
        span = pl.ds(GI[k], GI[k + 1] - GI[k])
        return pltpu.make_async_remote_copy(
            ts_in.at[aux_peer(r), span], tr_in.at[a, span], s2s.at[k, r - 1], s2r.at[k, r - 1],
            device_id={"aux": aux_peer(r)}, device_id_type=MESH)

    def edge(side):
        return (has_right, right) if side == "R" else (has_left, left)

    def send_x(k, side, to):
        lo, hi = GX[k]
        ts, tr = (ts_r, tr_r) if side == "R" else (ts_l, tr_l)
        return pltpu.make_async_remote_copy(
            ts.at[to, pl.ds(lo, hi - lo)], tr.at[a, pl.ds(lo, hi - lo)], cs.at[k - FAST, to], cr.at[k - FAST, a],
            device_id={"ao": edge(side)[1], "aux": to}, device_id_type=MESH)

    def got_x(k, side, source):
        lo, hi = GX[k]
        ts, tr = (ts_r, tr_r) if side == "R" else (ts_l, tr_l)
        return pltpu.make_async_remote_copy(
            ts.at[source, pl.ds(lo, hi - lo)], tr.at[source, pl.ds(lo, hi - lo)],
            cs.at[k - FAST, source], cr.at[k - FAST, source],
            device_id={"ao": edge("L" if side == "R" else "R")[1], "aux": source}, device_id_type=MESH)

    def upper_place(i, j):
        return NBLK - 1 - i, W + i + j

    def lower_place(i, j):
        return j, W - 1 - i - j

    def summed(k, side):
        send_own(k, side).wait_recv()
        send_joined(k, 0, side).wait_recv()

    def inner_sums(k):
        summed(k, None)
        sums(k * EARLY, [(i, W + j - i - 1) for i, j in INNER_PART[k]], ts_in, GI[k])
        tr_in[a, GI[k]:GI[k + 1]] = ts_in[a, GI[k]:GI[k + 1]]
        for r in range(1, AUX):
            send_in(k, r).start()

    def edge_sums(k, side):
        summed(k, side)
        spot, ts = (upper_place, ts_r) if side == "R" else (lower_place, ts_l)
        sums(start_of(k, side), [spot(i, j) for i, j in tiles_of(k, side)], ts, GX[k][0])

        @pl.when(edge(side)[0])
        def _():
            for to in range(AUX):
                send_x(k, side, to).start()

    def place(tr, g0, places):
        for u, (m, e) in enumerate(places):
            g, v = g0 + u // 4, u % 4
            pieces = [tr[source, g, :, v * SL:(v + 1) * SL].astype(jnp.float32) for source in range(AUX)]
            out_ref[m, e] = jnp.concatenate(pieces, axis=1)

    def inner_place(k):
        for r in range(1, AUX):
            send_in(k, r).wait_recv()
        place(tr_in, GI[k], [(j, W - (j - i)) for i, j in INNER_PART[k]])

    def edge_place(k, side):
        @pl.when(has_left if side == "R" else has_right)
        def _():
            for source in range(AUX):
                got_x(k, side, source).wait_recv()

        spot, tr = (lower_place, tr_r) if side == "R" else (upper_place, tr_l)
        place(tr, GX[k][0], [spot(i, j) for i, j in tiles_of(k, side)])

    def tail_to_right(to):
        return pltpu.make_async_remote_copy(
            tail_r.at[to], tail_r_in.at[a], cs.at[3, to], cr.at[3, a],
            device_id={"ao": right, "aux": to}, device_id_type=MESH)

    def tail_to_left(to):
        return pltpu.make_async_remote_copy(
            tail_l.at[to], tail_l_in.at[a], cs.at[3, to], cr.at[3, a],
            device_id={"ao": left, "aux": to}, device_id_type=MESH)

    def tail_from_left(source):
        return pltpu.make_async_remote_copy(
            tail_r.at[source], tail_r_in.at[source], cs.at[3, source], cr.at[3, source],
            device_id={"ao": left, "aux": source}, device_id_type=MESH)

    def tail_from_right(source):
        return pltpu.make_async_remote_copy(
            tail_l.at[source], tail_l_in.at[source], cs.at[3, source], cr.at[3, source],
            device_id={"ao": right, "aux": source}, device_id_type=MESH)

    def tail_out(side, to):
        return tail_to_right(to) if side == "R" else tail_to_left(to)

    def tail_send(side):
        for r in range(1, AUX):
            send_tail(r, side).start()

        @pl.when(edge(side)[0])
        def _():
            for to in range(AUX):
                tail_out(side, to).start()

    def tail_finish(side, other):
        for r in range(1, AUX):
            send_tail(r, side).wait_recv()
        spot = upper_place if side == "R" else lower_place
        for u, (i, j) in enumerate(tiles_of(LAST, side)):
            value = part[a, start_of(LAST, side) + u].astype(jnp.float32)
            for r in range(1, AUX):
                value = value + tail_in[r - 1, u].astype(jnp.float32)
            out_ref[spot(i, j)] = value

        @pl.when(edge(side)[0])
        def _():
            for source in range(AUX):
                (tail_from_left if other == "R" else tail_from_right)(source).wait_recv()

        spot, arrived = (lower_place, tail_r_in) if other == "R" else (upper_place, tail_l_in)
        for u, (i, j) in enumerate(tiles_of(LAST, other)):
            value = arrived[0, u].astype(jnp.float32)
            for source in range(1, AUX):
                value = value + arrived[source, u].astype(jnp.float32)
            out_ref[spot(i, j)] = value

    def by_side(step):
        @pl.when(even)
        def _():
            step("R", "L")

        @pl.when(jnp.logical_not(even))
        def _():
            step("L", "R")

    def fast_step(fast, slow):
        for b in range(3):
            cross(fast, b, False)

    def slow_step(b):
        def step(fast, slow):
            cross(slow, b, True)
            if b < 2:
                alpha(SLOW0 + b, slow)
            else:
                tail_send(slow)
        return step

    by_side(fast_step)
    beta(0, None)
    relay(1)
    by_side(lambda fast, slow: alpha(FAST, fast))
    by_side(slow_step(0))
    relay(2)
    beta(1, None)
    by_side(lambda fast, slow: beta(FAST, fast))
    by_side(slow_step(1))
    by_side(lambda fast, slow: beta(SLOW0, slow))
    inner_sums(0)
    inner_sums(1)
    by_side(lambda fast, slow: beta(SLOW1, slow))
    by_side(lambda fast, slow: edge_sums(FAST, fast))
    by_side(lambda fast, slow: edge_sums(SLOW0, slow))
    by_side(slow_step(2))
    by_side(lambda fast, slow: edge_sums(SLOW1, slow))
    inner_place(0)
    inner_place(1)
    by_side(lambda fast, slow: edge_place(FAST, slow))
    by_side(lambda fast, slow: edge_place(SLOW0, fast))
    by_side(lambda fast, slow: edge_place(SLOW1, fast))
    by_side(lambda fast, slow: tail_finish(slow, fast))

    def drain(fast, slow):
        for k, side in enumerate((None, None, fast, slow, slow)):
            send_own(k, side).wait_send()

            @pl.when(outer)
            def _():
                send_far(k, side).wait_send()

            @pl.when(jnp.logical_not(outer))
            def _():
                for h in range(2):
                    send_joined(k, h, side).wait_send()

        for r in range(1, AUX):
            send_tail(r, slow).wait_send()
        for k, side in ((FAST, fast), (SLOW0, slow), (SLOW1, slow)):
            @pl.when(edge(side)[0])
            def _():
                for to in range(AUX):
                    send_x(k, side, to).wait_send()

        @pl.when(edge(slow)[0])
        def _():
            for to in range(AUX):
                tail_out(slow, to).wait_send()

    by_side(drain)
    for r in range(1, AUX):
        for k in range(2):
            send_in(k, r).wait_send()

    @pl.when(has_right)
    def _():
        mask_copy.wait_send()

    for b in range(3):
        @pl.when(near_right)
        def _():
            to_right(b).wait_send()

        @pl.when(near_left)
        def _():
            to_left(b).wait_send()

        @pl.when(at_seam)
        def _():
            for p in range(PATHS):
                seam_out(b, p).wait_send()

        for p in range(1, PATHS):
            @pl.when(is_relay(p))
            def _():
                relay_out(b, p).wait_send()


def body(half_transformed, pair_mask):
    flat = half_transformed.reshape(-1, NBLK * BS)
    rows = flat.shape[0]
    bf16 = jnp.bfloat16
    dma = pltpu.SemaphoreType.DMA
    return pl.pallas_call(
        kernel,
        out_shape=jax.ShapeDtypeStruct((NBLK, 2 * W, SL, BS), jnp.float32),
        in_specs=[pl.BlockSpec(memory_space=pl.ANY)] * 2,
        out_specs=pl.BlockSpec(memory_space=pltpu.VMEM),
        scratch_shapes=[
            pltpu.VMEM((rows, NBLK * BS), bf16),
            pltpu.VMEM((rows // KC, NBLK * BS, KC), bf16),
            pltpu.VMEM((3, rows, 2 * BS), bf16),
            pltpu.VMEM((3, max(CUTS[p + 1] - CUTS[p] for p in range(1, PATHS)), BS), bf16),
            pltpu.VMEM((sum(INNER_M) * BS, 2 * BS), jnp.float32),
            pltpu.VMEM((AUX, N_ALL, SL, BS), bf16),
            pltpu.VMEM((N_ALL, SL, BS), bf16),
            pltpu.VMEM((2, N_ALL, SL, BS), bf16),
            pltpu.VMEM((2, N_ALL, SL, BS), bf16),
            pltpu.VMEM((N_ALL, SL, BS), bf16),
            pltpu.VMEM((AUX - 1, len(RIGHT[2]), SL, BS), bf16),
            pltpu.VMEM((AUX, GI[2], SL, BS), bf16),
            pltpu.VMEM((AUX, 3, SL, BS), bf16),
            pltpu.VMEM((AUX, 3, SL, BS), bf16),
            pltpu.VMEM((AUX, GI[2], SL, BS), bf16),
            pltpu.VMEM((AUX, 3, SL, BS), bf16),
            pltpu.VMEM((AUX, 3, SL, BS), bf16),
            pltpu.VMEM((AUX, len(RIGHT[2]), SL, BS), bf16),
            pltpu.VMEM((AUX, len(LEFT[2]), SL, BS), bf16),
            pltpu.VMEM((AUX, len(RIGHT[2]), SL, BS), bf16),
            pltpu.VMEM((AUX, len(LEFT[2]), SL, BS), bf16),
            pltpu.VMEM((NBLK, W), jnp.int32),
            pltpu.VMEM((NBLK, W), jnp.int32),
            dma((rows // KC,)), dma,
            dma((2, 3)), dma((2, 3)),
            dma((PATHS, 3)), dma((PATHS, 3)), dma((3,)), dma((3,)),
            dma, dma,
            dma((5,)), dma((5,)),
            dma((5,)), dma((5,)),
            dma((5, 2)), dma((5,)),
            dma((AUX - 1,)), dma((AUX - 1,)),
            dma((2, AUX - 1)), dma((2, AUX - 1)),
            dma((4, AUX)), dma((4, AUX)),
        ],
        compiler_params=pltpu.CompilerParams(
            collective_id=0, has_side_effects=True, vmem_limit_bytes=48 << 20),
        cost_estimate=pl.CostEstimate(flops=8 << 30, bytes_accessed=16 << 20, transcendentals=0),
    )(flat, pair_mask)


def solution(mesh):
    return jax.shard_map(
        body,
        mesh=mesh,
        in_specs=(P("aux", None, "ao"), P("ao", None)),
        out_specs=P("ao", None, "aux", None),
        check_vma=False,
    )
```

```python
import functools

import jax
import jax.numpy as jnp
from jax import lax
from jax.experimental import pallas as pl
from jax.experimental.pallas import tpu as pltpu
from jax.sharding import PartitionSpec as P

MESH = pl.DeviceIdType.MESH
BS = 128
W = 6
NBLK = 8
AUX = 4
SL = BS // AUX
KC = 1024
SEAM = 31
RELAY = [6, 14, 22, 0]
CUTS = [0, 640, 1536, 2560, 3456, 4096]
PATHS = len(RELAY) + 1

INNER = [(i, j) for j in range(1, NBLK) for i in range(max(0, j - W), j)]
INNER_M = [1, 3, 5, 7]
INNER_OFF = [0, 1, 4, 9]
RIGHT = [[(i, b) for i in range(b, W - b)] for b in range(3)]
LEFT = [[(b, j) for j in range(b + 1, W - b)] for b in range(3)]
def groups_of(count):
    return (count + 3) // 4


EARLY = 15
INNER_PART = [INNER[:EARLY], INNER[EARLY:]]
FAST, SLOW0, SLOW1, LAST = 2, 3, 4, 5
GI = [0, groups_of(EARLY), groups_of(EARLY) + groups_of(len(INNER) - EARLY)]
SIDES = {"R": RIGHT, "L": LEFT}
BASE = {"R": len(INNER), "L": len(INNER) + sum(map(len, RIGHT))}
N_ALL = BASE["L"] + sum(map(len, LEFT))
GX = {FAST: (0, 3), SLOW0: (0, 2), SLOW1: (2, 3)}


def tiles_of(k, side):
    if k < FAST:
        return INNER_PART[k]
    if k == FAST:
        return sum(SIDES[side], [])
    return SIDES[side][k - SLOW0]


def start_of(k, side):
    if k < FAST:
        return k * EARLY
    if k == FAST:
        return BASE[side]
    return BASE[side] + sum(map(len, SIDES[side][:k - SLOW0]))


def rows_of(side, b):
    return (2 + b, NBLK - b) if side == "R" else (1 + b, W - b)


def kernel(
    x_hbm, mask_hbm, out_ref,
    x, xt, hal, rel, acc, part, own_sum, far_sum, far_out, far_in, tail_in,
    ts_in, ts_r, ts_l, tr_in, tr_r, tr_l, tail_r, tail_l, tail_r_in, tail_l_in, mask_own, mask_prev,
    load_sem, mask_sem, hs, hr, ss, sr, rs, rr, ms, mr,
    os, orr, fs, fr, gs, gr, ds, dr, s2s, s2r, cs, cr,
):
    rows = x.shape[0]
    chunks = rows // KC
    n = lax.axis_index("ao")
    a = lax.axis_index("aux")
    n_ao = lax.axis_size("ao")
    fwd = n <= SEAM
    at_seam = (n == SEAM) | (n == SEAM + 1)
    last = n_ao - 1
    even = lax.rem(n, 2) == 0
    has_left = n > 0
    has_right = n < n_ao - 1
    pair = a + 1 - 2 * lax.rem(a, 2)
    outer = (a == 0) | (a == AUX - 1)
    other_half = jnp.where(a < 2, 2, 0)
    left = jnp.maximum(n - 1, 0)
    right = jnp.minimum(n + 1, n_ao - 1)

    def aux_peer(r):
        return lax.rem(a + r, AUX)

    barrier = pltpu.get_barrier_semaphore()
    for r in range(1, AUX):
        pl.semaphore_signal(barrier, 1, device_id={"aux": aux_peer(r)}, device_id_type=MESH)

    @pl.when(has_left)
    def _():
        for b in range(AUX):
            pl.semaphore_signal(barrier, 1, device_id={"ao": left, "aux": b}, device_id_type=MESH)

    @pl.when(has_right)
    def _():
        for b in range(AUX):
            pl.semaphore_signal(barrier, 1, device_id={"ao": right, "aux": b}, device_id_type=MESH)

    def relay_of(p):
        return jnp.where(fwd, RELAY[p - 1], last - RELAY[p - 1])

    def is_relay(p):
        return n == relay_of(p)

    relay_to = jnp.where(fwd, SEAM + 1, SEAM)
    relay_from = jnp.where(fwd, SEAM, SEAM + 1)
    extra = jnp.where(at_seam, PATHS - 1, 0)
    for p in range(1, PATHS):
        extra += jnp.where(is_relay(p), 1, 0)

        @pl.when(is_relay(p))
        def _():
            pl.semaphore_signal(barrier, 1, device_id={"ao": relay_from}, device_id_type=MESH)

        @pl.when(at_seam)
        def _():
            other = jnp.where(fwd, last - RELAY[p - 1], RELAY[p - 1])
            pl.semaphore_signal(barrier, 1, device_id={"ao": other}, device_id_type=MESH)

    def load(c):
        piece = pl.ds(pl.multiple_of(c * KC, KC), KC)
        return pltpu.make_async_copy(x_hbm.at[piece], x.at[piece], load_sem.at[c])

    for c in range(chunks):
        load(c).start()
    mask_load = pltpu.make_async_copy(mask_hbm, mask_own, mask_sem)
    mask_load.start()

    pl.semaphore_wait(
        barrier, AUX - 1 + AUX * (has_left.astype(jnp.int32) + has_right.astype(jnp.int32)) + extra)

    def to_left(b):
        return pltpu.make_async_remote_copy(
            x_hbm.at[:, pl.ds(b * BS, BS)], hal.at[b, :, pl.ds(0, BS)],
            hs.at[0, b], hr.at[0, b], device_id={"ao": left}, device_id_type=MESH)

    def to_right(b):
        return pltpu.make_async_remote_copy(
            x_hbm.at[:, pl.ds((NBLK - 1 - b) * BS, BS)], hal.at[b, :, pl.ds(BS, BS)],
            hs.at[1, b], hr.at[1, b], device_id={"ao": right}, device_id_type=MESH)

    def seam_span(p, lanes):
        return (pl.ds(CUTS[p], CUTS[p + 1] - CUTS[p]), pl.ds(pl.multiple_of(lanes, BS), BS))

    def parked(b, p):
        return rel.at[b, pl.ds(0, CUTS[p + 1] - CUTS[p])]

    def seam_out(b, p):
        source = x_hbm.at[seam_span(p, jnp.where(fwd, (NBLK - 1 - b) * BS, b * BS))]
        if p == 0:
            return pltpu.make_async_remote_copy(
                source, hal.at[(b,) + seam_span(p, jnp.where(fwd, BS, 0))],
                ss.at[p, b], sr.at[p, b], device_id={"ao": relay_to}, device_id_type=MESH)
        return pltpu.make_async_remote_copy(
            source, parked(b, p), ss.at[p, b], rr.at[b], device_id={"ao": relay_of(p)}, device_id_type=MESH)

    def relay_out(b, p):
        return pltpu.make_async_remote_copy(
            parked(b, p), hal.at[(b,) + seam_span(p, jnp.where(fwd, BS, 0))],
            rs.at[b], sr.at[p, b], device_id={"ao": relay_to}, device_id_type=MESH)

    def seam_in(b, p):
        return pltpu.make_async_remote_copy(
            parked(b, p), hal.at[(b,) + seam_span(p, jnp.where(fwd, 0, BS))],
            rs.at[b], sr.at[p, b], device_id={"ao": relay_to}, device_id_type=MESH)

    def relay(b):
        for p in range(1, PATHS):
            @pl.when(is_relay(p))
            def _():
                seam_out(b, p).wait_recv()
                relay_out(b, p).start()

    near_left = has_left & (n != SEAM + 1)
    near_right = has_right & (n != SEAM)
    mask_copy = pltpu.make_async_remote_copy(
        mask_own, mask_prev, ms, mr, device_id={"ao": right}, device_id_type=MESH)

    for b in range(3):
        @pl.when(at_seam)
        def _():
            for p in (1, 2, 4, 3, 0):
                seam_out(b, p).start()

        @pl.when(near_left)
        def _():
            to_left(b).start()

        @pl.when(near_right)
        def _():
            to_right(b).start()

    mask_load.wait()

    @pl.when(has_right)
    def _():
        mask_copy.start()

    @pl.when(jnp.logical_not(has_left))
    def _():
        hal[:, :, BS:] = jnp.zeros((3, rows, BS), hal.dtype)
        tr_r[...] = jnp.zeros_like(tr_r)
        tail_r_in[...] = jnp.zeros_like(tail_r_in)
        mask_prev[...] = jnp.zeros_like(mask_prev)

    @pl.when(jnp.logical_not(has_right))
    def _():
        hal[:, :, :BS] = jnp.zeros((3, rows, BS), hal.dtype)
        tr_l[...] = jnp.zeros_like(tr_l)
        tail_l_in[...] = jnp.zeros_like(tail_l_in)

    acc[...] = jnp.zeros_like(acc)

    def inner_step(turned, wide, first):
        def step(c, carry):
            if first:
                load(c).wait()
            piece = pl.ds(pl.multiple_of(c * KC, KC), KC)
            for b in turned:
                xt[c, b * BS:(b + 1) * BS, :] = x[piece, b * BS:(b + 1) * BS].T
            for q in wide:
                lhs = xt[c, 0:INNER_M[q] * BS, :]
                rhs = x[piece, 2 * q * BS:(2 * q + 2) * BS]
                where = slice(INNER_OFF[q] * BS, (INNER_OFF[q] + INNER_M[q]) * BS)
                acc[where, :] += jnp.dot(lhs, rhs, preferred_element_type=jnp.float32)
            return carry

        lax.fori_loop(0, chunks, step, 0)

    def scaled(tile, keep):
        return (tile * (keep > 0).astype(jnp.float32)).astype(part.dtype)

    def put(tile, keep, t):
        part[:, t] = scaled(tile, keep).reshape(AUX, SL, BS)

    def put_inner(k):
        for u, (i, j) in enumerate(INNER_PART[k]):
            row = (INNER_OFF[j // 2] + i) * BS
            col = (j % 2) * BS
            put(acc[row:row + BS, col:col + BS], mask_own[i:i + 1, j - i - 1:j - i], k * EARLY + u)

    def span_of(k, side):
        return pl.ds(start_of(k, side), len(tiles_of(k, side)))

    def send_far(k, side):
        return pltpu.make_async_remote_copy(
            part.at[pl.ds(other_half, 2), span_of(k, side)], far_sum.at[:, span_of(k, side)],
            fs.at[k], fr.at[k], device_id={"aux": pair}, device_id_type=MESH)

    def send_own(k, side):
        return pltpu.make_async_remote_copy(
            part.at[pair, span_of(k, side)], own_sum.at[span_of(k, side)],
            os.at[k], orr.at[k], device_id={"aux": pair}, device_id_type=MESH)

    def send_joined(k, h, side):
        return pltpu.make_async_remote_copy(
            far_out.at[h, span_of(k, side)], far_in.at[span_of(k, side)],
            gs.at[k, h], gr.at[k], device_id={"aux": other_half + h}, device_id_type=MESH)

    def alpha(k, side):
        @pl.when(outer)
        def _():
            send_far(k, side).start()

        send_own(k, side).start()

    def beta(k, side):
        @pl.when(jnp.logical_not(outer))
        def _():
            send_far(k, side).wait_recv()
            for h in range(2):
                for t in range(start_of(k, side), start_of(k, side) + len(tiles_of(k, side))):
                    far_out[h, t] = (
                        part[other_half + h, t].astype(jnp.float32) + far_sum[h, t].astype(jnp.float32)
                    ).astype(part.dtype)
                send_joined(k, h, side).start()

    def send_tail(r, side):
        count = len(tiles_of(LAST, side))
        return pltpu.make_async_remote_copy(
            part.at[aux_peer(r), span_of(LAST, side)], tail_in.at[r - 1, pl.ds(0, count)],
            ds.at[r - 1], dr.at[r - 1], device_id={"aux": aux_peer(r)}, device_id_type=MESH)

    inner_step(range(0, 5), range(0, 3), True)
    put_inner(0)
    alpha(0, None)
    relay(0)
    inner_step(range(5, NBLK), range(3, 4), False)
    put_inner(1)
    alpha(1, None)

    def arrive(side, b):
        if side == "R":
            @pl.when(near_right)
            def _():
                to_left(b).wait_recv()
        else:
            @pl.when(near_left)
            def _():
                to_right(b).wait_recv()

            if b == 0:
                @pl.when(has_left)
                def _():
                    mask_copy.wait_recv()

    def cross(side, b, slow):
        arrive(side, b)
        if slow:
            @pl.when(at_seam)
            def _():
                for p in range(PATHS):
                    seam_in(b, p).wait_recv()

        lo, hi = rows_of(side, b)
        size = (hi - lo) * BS
        lanes = slice(0, BS) if side == "R" else slice(BS, 2 * BS)
        acc[0:size, 0:BS] = jnp.zeros((size, BS), jnp.float32)

        def step(c, carry):
            piece = pl.ds(pl.multiple_of(c * KC, KC), KC)
            acc[0:size, 0:BS] += jnp.dot(
                xt[c, lo * BS:hi * BS, :], hal[b, piece, lanes], preferred_element_type=jnp.float32)
            return carry

        lax.fori_loop(0, chunks, step, 0)
        t0 = start_of(SLOW0 + b, side)
        for u, (i, j) in enumerate(SIDES[side][b]):
            far = NBLK - 1 - i
            row = ((far if side == "R" else j) - lo) * BS
            tile = acc[row:row + BS, 0:BS]
            keep = (mask_own if side == "R" else mask_prev)[far:far + 1, i + j:i + j + 1]
            put(tile, keep, t0 + u)
            if slow and b == 2:
                (tail_r if side == "R" else tail_l)[:, u] = scaled(tile.T, keep).reshape(AUX, SL, BS)

    def total(t):
        return part[a, t].astype(jnp.float32) + own_sum[t].astype(jnp.float32) + far_in[t].astype(jnp.float32)

    def turn(values, ts, g):
        values = values + [jnp.zeros((SL, BS), jnp.float32)] * (4 - len(values))
        ts[:, g] = jnp.concatenate(values, axis=0).T.astype(ts.dtype).reshape(AUX, SL, BS)

    def sums(t0, places, ts, g0):
        for g in range(groups_of(len(places))):
            values = []
            for u, (m, e) in enumerate(places[4 * g:4 * g + 4]):
                value = total(t0 + 4 * g + u)
                out_ref[m, e] = value
                values.append(value)
            turn(values, ts, g0 + g)

    def send_in(k, r):
        span = pl.ds(GI[k], GI[k + 1] - GI[k])
        return pltpu.make_async_remote_copy(
            ts_in.at[aux_peer(r), span], tr_in.at[a, span], s2s.at[k, r - 1], s2r.at[k, r - 1],
            device_id={"aux": aux_peer(r)}, device_id_type=MESH)

    def edge(side):
        return (has_right, right) if side == "R" else (has_left, left)

    def send_x(k, side, to):
        lo, hi = GX[k]
        ts, tr = (ts_r, tr_r) if side == "R" else (ts_l, tr_l)
        return pltpu.make_async_remote_copy(
            ts.at[to, pl.ds(lo, hi - lo)], tr.at[a, pl.ds(lo, hi - lo)], cs.at[k - FAST, to], cr.at[k - FAST, a],
            device_id={"ao": edge(side)[1], "aux": to}, device_id_type=MESH)

    def got_x(k, side, source):
        lo, hi = GX[k]
        ts, tr = (ts_r, tr_r) if side == "R" else (ts_l, tr_l)
        return pltpu.make_async_remote_copy(
            ts.at[source, pl.ds(lo, hi - lo)], tr.at[source, pl.ds(lo, hi - lo)],
            cs.at[k - FAST, source], cr.at[k - FAST, source],
            device_id={"ao": edge("L" if side == "R" else "R")[1], "aux": source}, device_id_type=MESH)

    def upper_place(i, j):
        return NBLK - 1 - i, W + i + j

    def lower_place(i, j):
        return j, W - 1 - i - j

    def summed(k, side):
        send_own(k, side).wait_recv()
        send_joined(k, 0, side).wait_recv()

    def inner_sums(k):
        summed(k, None)
        sums(k * EARLY, [(i, W + j - i - 1) for i, j in INNER_PART[k]], ts_in, GI[k])
        tr_in[a, GI[k]:GI[k + 1]] = ts_in[a, GI[k]:GI[k + 1]]
        for r in range(1, AUX):
            send_in(k, r).start()

    def edge_sums(k, side):
        summed(k, side)
        spot, ts = (upper_place, ts_r) if side == "R" else (lower_place, ts_l)
        sums(start_of(k, side), [spot(i, j) for i, j in tiles_of(k, side)], ts, GX[k][0])

        @pl.when(edge(side)[0])
        def _():
            for to in range(AUX):
                send_x(k, side, to).start()

    def place(tr, g0, places):
        for u, (m, e) in enumerate(places):
            g, v = g0 + u // 4, u % 4
            pieces = [tr[source, g, :, v * SL:(v + 1) * SL].astype(jnp.float32) for source in range(AUX)]
            out_ref[m, e] = jnp.concatenate(pieces, axis=1)

    def inner_place(k):
        for r in range(1, AUX):
            send_in(k, r).wait_recv()
        place(tr_in, GI[k], [(j, W - (j - i)) for i, j in INNER_PART[k]])

    def edge_place(k, side):
        @pl.when(has_left if side == "R" else has_right)
        def _():
            for source in range(AUX):
                got_x(k, side, source).wait_recv()

        spot, tr = (lower_place, tr_r) if side == "R" else (upper_place, tr_l)
        place(tr, GX[k][0], [spot(i, j) for i, j in tiles_of(k, side)])

    def tail_to_right(to):
        return pltpu.make_async_remote_copy(
            tail_r.at[to], tail_r_in.at[a], cs.at[3, to], cr.at[3, a],
            device_id={"ao": right, "aux": to}, device_id_type=MESH)

    def tail_to_left(to):
        return pltpu.make_async_remote_copy(
            tail_l.at[to], tail_l_in.at[a], cs.at[3, to], cr.at[3, a],
            device_id={"ao": left, "aux": to}, device_id_type=MESH)

    def tail_from_left(source):
        return pltpu.make_async_remote_copy(
            tail_r.at[source], tail_r_in.at[source], cs.at[3, source], cr.at[3, source],
            device_id={"ao": left, "aux": source}, device_id_type=MESH)

    def tail_from_right(source):
        return pltpu.make_async_remote_copy(
            tail_l.at[source], tail_l_in.at[source], cs.at[3, source], cr.at[3, source],
            device_id={"ao": right, "aux": source}, device_id_type=MESH)

    def tail_out(side, to):
        return tail_to_right(to) if side == "R" else tail_to_left(to)

    def tail_send(side):
        for r in range(1, AUX):
            send_tail(r, side).start()

        @pl.when(edge(side)[0])
        def _():
            for to in range(AUX):
                tail_out(side, to).start()

    def tail_finish(side, other):
        for r in range(1, AUX):
            send_tail(r, side).wait_recv()
        spot = upper_place if side == "R" else lower_place
        for u, (i, j) in enumerate(tiles_of(LAST, side)):
            value = part[a, start_of(LAST, side) + u].astype(jnp.float32)
            for r in range(1, AUX):
                value = value + tail_in[r - 1, u].astype(jnp.float32)
            out_ref[spot(i, j)] = value

        @pl.when(edge(side)[0])
        def _():
            for source in range(AUX):
                (tail_from_left if other == "R" else tail_from_right)(source).wait_recv()

        spot, arrived = (lower_place, tail_r_in) if other == "R" else (upper_place, tail_l_in)
        for u, (i, j) in enumerate(tiles_of(LAST, other)):
            value = arrived[0, u].astype(jnp.float32)
            for source in range(1, AUX):
                value = value + arrived[source, u].astype(jnp.float32)
            out_ref[spot(i, j)] = value

    def by_side(step):
        @pl.when(even)
        def _():
            step("R", "L")

        @pl.when(jnp.logical_not(even))
        def _():
            step("L", "R")

    def fast_step(fast, slow):
        for b in range(3):
            cross(fast, b, False)

    def slow_step(b):
        def step(fast, slow):
            cross(slow, b, True)
            if b < 2:
                alpha(SLOW0 + b, slow)
            else:
                tail_send(slow)
        return step

    by_side(fast_step)
    beta(0, None)
    relay(1)
    by_side(lambda fast, slow: alpha(FAST, fast))
    by_side(slow_step(0))
    relay(2)
    beta(1, None)
    by_side(lambda fast, slow: beta(FAST, fast))
    by_side(slow_step(1))
    by_side(lambda fast, slow: beta(SLOW0, slow))
    inner_sums(0)
    inner_sums(1)
    by_side(lambda fast, slow: beta(SLOW1, slow))
    by_side(lambda fast, slow: edge_sums(FAST, fast))
    by_side(lambda fast, slow: edge_sums(SLOW0, slow))
    by_side(slow_step(2))
    by_side(lambda fast, slow: edge_sums(SLOW1, slow))
    inner_place(0)
    inner_place(1)
    by_side(lambda fast, slow: edge_place(FAST, slow))
    by_side(lambda fast, slow: edge_place(SLOW0, fast))
    by_side(lambda fast, slow: edge_place(SLOW1, fast))
    by_side(lambda fast, slow: tail_finish(slow, fast))

    def drain(fast, slow):
        for k, side in enumerate((None, None, fast, slow, slow)):
            send_own(k, side).wait_send()

            @pl.when(outer)
            def _():
                send_far(k, side).wait_send()

            @pl.when(jnp.logical_not(outer))
            def _():
                for h in range(2):
                    send_joined(k, h, side).wait_send()

        for r in range(1, AUX):
            send_tail(r, slow).wait_send()
        for k, side in ((FAST, fast), (SLOW0, slow), (SLOW1, slow)):
            @pl.when(edge(side)[0])
            def _():
                for to in range(AUX):
                    send_x(k, side, to).wait_send()

        @pl.when(edge(slow)[0])
        def _():
            for to in range(AUX):
                tail_out(slow, to).wait_send()

    by_side(drain)
    for r in range(1, AUX):
        for k in range(2):
            send_in(k, r).wait_send()

    @pl.when(has_right)
    def _():
        mask_copy.wait_send()

    for b in range(3):
        @pl.when(near_right)
        def _():
            to_right(b).wait_send()

        @pl.when(near_left)
        def _():
            to_left(b).wait_send()

        @pl.when(at_seam)
        def _():
            for p in range(PATHS):
                seam_out(b, p).wait_send()

        for p in range(1, PATHS):
            @pl.when(is_relay(p))
            def _():
                relay_out(b, p).wait_send()


def body(half_transformed, pair_mask):
    flat = half_transformed.reshape(-1, NBLK * BS)
    rows = flat.shape[0]
    bf16 = jnp.bfloat16
    dma = pltpu.SemaphoreType.DMA
    return pl.pallas_call(
        kernel,
        out_shape=jax.ShapeDtypeStruct((NBLK, 2 * W, SL, BS), jnp.float32),
        in_specs=[pl.BlockSpec(memory_space=pl.ANY)] * 2,
        out_specs=pl.BlockSpec(memory_space=pltpu.VMEM),
        scratch_shapes=[
            pltpu.VMEM((rows, NBLK * BS), bf16),
            pltpu.VMEM((rows // KC, NBLK * BS, KC), bf16),
            pltpu.VMEM((3, rows, 2 * BS), bf16),
            pltpu.VMEM((3, max(CUTS[p + 1] - CUTS[p] for p in range(1, PATHS)), BS), bf16),
            pltpu.VMEM((sum(INNER_M) * BS, 2 * BS), jnp.float32),
            pltpu.VMEM((AUX, N_ALL, SL, BS), bf16),
            pltpu.VMEM((N_ALL, SL, BS), bf16),
            pltpu.VMEM((2, N_ALL, SL, BS), bf16),
            pltpu.VMEM((2, N_ALL, SL, BS), bf16),
            pltpu.VMEM((N_ALL, SL, BS), bf16),
            pltpu.VMEM((AUX - 1, len(RIGHT[2]), SL, BS), bf16),
            pltpu.VMEM((AUX, GI[2], SL, BS), bf16),
            pltpu.VMEM((AUX, 3, SL, BS), bf16),
            pltpu.VMEM((AUX, 3, SL, BS), bf16),
            pltpu.VMEM((AUX, GI[2], SL, BS), bf16),
            pltpu.VMEM((AUX, 3, SL, BS), bf16),
            pltpu.VMEM((AUX, 3, SL, BS), bf16),
            pltpu.VMEM((AUX, len(RIGHT[2]), SL, BS), bf16),
            pltpu.VMEM((AUX, len(LEFT[2]), SL, BS), bf16),
            pltpu.VMEM((AUX, len(RIGHT[2]), SL, BS), bf16),
            pltpu.VMEM((AUX, len(LEFT[2]), SL, BS), bf16),
            pltpu.VMEM((NBLK, W), jnp.int32),
            pltpu.VMEM((NBLK, W), jnp.int32),
            dma((rows // KC,)), dma,
            dma((2, 3)), dma((2, 3)),
            dma((PATHS, 3)), dma((PATHS, 3)), dma((3,)), dma((3,)),
            dma, dma,
            dma((5,)), dma((5,)),
            dma((5,)), dma((5,)),
            dma((5, 2)), dma((5,)),
            dma((AUX - 1,)), dma((AUX - 1,)),
            dma((2, AUX - 1)), dma((2, AUX - 1)),
            dma((4, AUX)), dma((4, AUX)),
        ],
        compiler_params=pltpu.CompilerParams(
            collective_id=0, has_side_effects=True, vmem_limit_bytes=48 << 20),
        cost_estimate=pl.CostEstimate(flops=8 << 30, bytes_accessed=16 << 20, transcendentals=0),
    )(flat, pair_mask)


def solution(mesh):
    return jax.shard_map(
        body,
        mesh=mesh,
        in_specs=(P("aux", None, "ao"), P("ao", None)),
        out_specs=P("ao", None, "aux", None),
        check_vma=False,
    )
```
